32 devices in a mesh: patch: 8 (over y, x, core), slab: 4 (over z).
Axes of the slice: x: 2, y: 2, z: 4, core: 2. Of those that a mesh axis runs over, the one named last changes fastest.
Arguments:
- history: bfloat16 [128, 256, 128], P('patch', 'slab'), may hold values from -6 to 6
- interp_weights: bfloat16 [128, 32, 4], P('patch'), may hold values from -3 to 3
- pair_table: int32 [128, 32, 3], P('patch'), may hold values from 0 to 252, as said below
- coupling: bfloat16 [128, 32, 128, 128], P('patch', 'slab'), may hold values from -0.09375 to 0.09375
- self_inverse: bfloat16 [128, 128, 128], P('patch'), may hold values from -0.5 to 0.5
- incident: float32 [128, 4, 128], P('patch'), may hold values from -6 to 6
Outputs:
- amplitudes: bfloat16 [128, 4, 128], P('patch')
The draws below stay inside these ranges and needn't reach their ends.
Inputs may be any that keep to these rules, and one draw needn't show every extreme that they name: pair_table[p, k] holds the observer patch (0 to 127), the first delay step (1 to 252) and the band width (1 to 4) of the k-th interaction whose sources are patch p's.
All inputs are finite; a program needn't handle non-finite values.
Results may differ from the reference program's by a relative error of at most 0.008.
Values may be sent and summed in bfloat16 or wider, within the bound.
A program may use at most 64 MiB of HBM per device.

```python
import jax
import jax.numpy as jnp
from jax import lax

SRC = 128
HIST = 256
WMAX = 4
STEPS = 4
PAIRS = 32
PATCHES = 128


def draw_pair_table(key, part):
    keys = jax.random.split(jax.random.fold_in(key, 7), 5)
    observer = jax.random.randint(keys[0], (PATCHES, PAIRS), 0, PATCHES)
    near_delay = jax.random.randint(keys[1], (PATCHES, PAIRS), 1, 2)
    far_delay = jax.random.randint(keys[2], (PATCHES, PAIRS), 1, HIST - WMAX + 1)
    picker = jax.random.randint(keys[3], (PATCHES, PAIRS), 0, 4)
    first_delay = jnp.where(picker == 0, near_delay, far_delay)
    band_width = jax.random.randint(keys[4], (PATCHES, PAIRS), 1, WMAX + 1)
    observer = observer.at[0, 0].set(PATCHES - 1)
    first_delay = first_delay.at[0, 1].set(HIST - WMAX)
    return jnp.stack([observer, first_delay, band_width], axis=-1).astype(jnp.int32)


def shard_levels(stream_key, shape, shards, smallest, largest):
    def one(axis_at, blocks):
        steps = jax.random.uniform(jax.random.fold_in(jax.random.fold_in(stream_key, 6), axis_at), (blocks,), jnp.float32, smallest / len(shards), largest / len(shards))
        return jnp.repeat(jnp.exp(steps), shape[axis_at] // blocks).reshape((-1,) + (1,) * (len(shape) - axis_at - 1))

    gain = one(*shards[0])
    for cut in shards[1:]:
        gain = gain * one(*cut)
    return gain


def bell_draw(stream_key, dims, deviation, limit, cuts=(), kind=jnp.bfloat16):
    level = shard_levels(stream_key, dims, cuts, -0.22, 0.18) if cuts else 1.0
    values = jax.random.normal(stream_key, dims, jnp.float32) * deviation * level
    return jnp.minimum(jnp.maximum(values, -limit), limit).astype(kind)


def setup_inputs(seed: int = 0) -> dict:
    seeds = jax.random.split(jax.random.key(seed), 7)
    return {
        "history": bell_draw(seeds[0], (PATCHES, HIST, SRC), 1.0, 6.0, ((0, 8), (1, 4))),
        "interp_weights": bell_draw(seeds[1], (PATCHES, PAIRS, WMAX), 1.0, 3.0, ((0, 8),)),
        "pair_table": draw_pair_table(jax.random.fold_in(seeds[6], 71), 0),
        "coupling": bell_draw(seeds[3], (PATCHES, PAIRS, SRC, SRC), (SRC * PAIRS) ** -0.5, 0.09375, ((0, 8), (1, 4))),
        "self_inverse": bell_draw(seeds[4], (PATCHES, SRC, SRC), SRC ** -0.5, 0.5, ((0, 8),)),
        "incident": bell_draw(seeds[5], (PATCHES, STEPS, SRC), 1.0, 6.0, ((0, 8),), jnp.float32),
    }


def reference(history, interp_weights, pair_table, coupling, self_inverse, incident):
    observer = pair_table[:, :, 0]
    first_delay = pair_table[:, :, 1]
    band_width = pair_table[:, :, 2]
    tap_index = jnp.arange(WMAX, dtype=jnp.int32)
    weights = jnp.where(tap_index[None, None, :] < band_width[:, :, None], interp_weights.astype(jnp.float32), jnp.float32(0.0))
    new_amps = jnp.zeros((PATCHES, STEPS, SRC), jnp.bfloat16)
    patch_rows = jnp.arange(PATCHES, dtype=jnp.int32)[:, None, None]
    for time_step in range(STEPS):
        timeline = jnp.concatenate([new_amps[:, ::-1], history], axis=1).astype(jnp.float32)
        position = (first_delay[:, :, None] + tap_index[None, None, :] - time_step - 1 + STEPS).astype(jnp.int32)
        picked = timeline[patch_rows, position]
        driven = jnp.sum(weights[..., None] * picked, axis=2).astype(jnp.bfloat16)

        def apply_one(pieces):
            matrices, vectors = pieces
            return jnp.einsum('kij,kj->ki', matrices.astype(jnp.float32), vectors.astype(jnp.float32))

        coupled = lax.map(apply_one, (coupling, driven))
        scattered = jax.ops.segment_sum(coupled.reshape(-1, SRC), observer.reshape(-1), num_segments=PATCHES)
        drive = (incident[:, time_step] - scattered).astype(jnp.bfloat16)
        amplitude = jnp.einsum('pij,pj->pi', self_inverse.astype(jnp.float32), drive.astype(jnp.float32)).astype(jnp.bfloat16)
        new_amps = new_amps.at[:, time_step].set(amplitude)
    return new_amps
```

```python
import functools

import jax
import jax.numpy as jnp
from jax import lax
from jax.experimental import pallas as pl
from jax.experimental.pallas import tpu as pltpu
from jax.sharding import PartitionSpec as P

WMAX = 4
STEPS = 4
MESH = pl.DeviceIdType.MESH
F32 = jnp.float32
BF16 = jnp.bfloat16


def nt_dot(x, m):
    return lax.dot_general(x, m, (((1,), (1,)), ((), ())), preferred_element_type=F32)


def own_blocks(x, m):
    rows, src = x.shape
    full = nt_dot(x.astype(BF16), m)
    row = lax.broadcasted_iota(jnp.int32, (rows, src), 0)
    out = full[:, :src]
    for r in range(1, rows):
        out = jnp.where(row == r, full[:, r * src : (r + 1) * src], out)
    return out


def march(
    n_patch,
    n_slab,
    hist_ref,
    w_ref,
    pt_ref,
    coup_hbm,
    inv_hbm,
    inc_ref,
    out_ref,
    coup,
    inv,
    wm,
    recent_w,
    onehot,
    inc,
    amps,
    pre,
    coupled,
    hsend,
    hrecv,
    fsend,
    frecv,
    zbuf,
    local_sem,
    h_send_sem,
    h_recv_sem,
    f_send_sem,
    f_recv_sem,
    z_send_sem,
    z_recv_sem,
):
    patches, slab_len, src = hist_ref.shape
    pairs = pt_ref.shape[1]
    loc = pairs // n_slab
    rows = patches * loc
    total = n_patch * patches
    me = lax.axis_index("patch")
    slab = lax.axis_index("slab")

    def patch_peer(off):
        return lax.rem(me + off, n_patch)

    def slab_peer(off):
        return lax.rem(slab + off, n_slab)

    barrier = pltpu.get_barrier_semaphore()
    for off in range(1, n_patch):
        pl.semaphore_signal(
            barrier, inc=1, device_id={"patch": patch_peer(off), "slab": slab}, device_id_type=MESH
        )
    for off in range(1, n_slab):
        pl.semaphore_signal(
            barrier, inc=1, device_id={"patch": me, "slab": slab_peer(off)}, device_id_type=MESH
        )

    parts = 4
    size = patches // parts
    loads = [
        pltpu.make_async_copy(
            coup_hbm.at[pl.ds(c * size, size)], coup.at[pl.ds(c * size, size)], local_sem.at[c]
        )
        for c in range(parts)
    ]
    loads.append(pltpu.make_async_copy(inv_hbm, inv, local_sem.at[parts]))
    for load in loads:
        load.start()

    lane = lax.broadcasted_iota(jnp.int32, (pairs, slab_len), 1) + (slab * slab_len + 1)
    tap = lax.broadcasted_iota(jnp.int32, (pairs, WMAX), 1)

    def stored_share(p, steps):
        table = pt_ref[p]
        weights = wm[p]
        shift = lane - table[:, 1:2]
        hits = []
        for step in steps:
            hit = jnp.zeros((pairs, slab_len), F32)
            for j in range(WMAX):
                hit = jnp.where(shift == j - step, weights[:, j : j + 1], hit)
            hits.append(hit)
        hit = hits[0] if len(hits) == 1 else jnp.concatenate(hits, axis=0)
        return jnp.dot(hit.astype(BF16), hist_ref[p], preferred_element_type=F32)

    def share_of_steps(steps):
        def two(i, carry):
            a = stored_share(2 * i, steps)
            b = stored_share(2 * i + 1, steps)
            at = pl.ds(pl.multiple_of(i * 2 * loc, 2 * loc), 2 * loc)
            for k, step in enumerate(steps):
                for d in range(n_slab):
                    r = k * pairs + d * loc
                    both = jnp.concatenate([a[r : r + loc], b[r : r + loc]], axis=0)
                    hsend[step, d, at, :] = both.astype(BF16)
            return carry

        lax.fori_loop(0, patches // 2, two, 0, unroll=True)

    def hist_copy(step, off):
        dest = slab_peer(off)
        return pltpu.make_async_remote_copy(
            src_ref=hsend.at[step, dest],
            dst_ref=hrecv.at[step, off],
            send_sem=h_send_sem.at[step, off],
            recv_sem=h_recv_sem.at[step, off],
            device_id={"patch": me, "slab": dest},
            device_id_type=MESH,
        )

    def field_copy(step, off):
        dest = patch_peer(off)
        return pltpu.make_async_remote_copy(
            src_ref=fsend.at[step, dest],
            dst_ref=frecv.at[step, off],
            send_sem=f_send_sem.at[step, off],
            recv_sem=f_recv_sem.at[step, off],
            device_id={"patch": dest, "slab": slab},
            device_id_type=MESH,
        )

    def slab_copy(step, off):
        return pltpu.make_async_remote_copy(
            src_ref=zbuf.at[step, 0],
            dst_ref=zbuf.at[step, off],
            send_sem=z_send_sem.at[step, off],
            recv_sem=z_recv_sem.at[step, off],
            device_id={"patch": me, "slab": slab_peer(off)},
            device_id_type=MESH,
        )

    for p in range(patches):
        wm[p] = jnp.where(tap < pt_ref[p][:, 2:3], w_ref[p].astype(F32), 0.0)
    share_of_steps([0])

    pl.semaphore_wait(barrier, n_patch + n_slab - 2)
    hist_copies = [hist_copy(0, off) for off in range(1, n_slab)]
    for copy in hist_copies:
        copy.start()

    share_of_steps(list(range(1, STEPS)))
    for step in range(1, STEPS):
        for off in range(1, n_slab):
            copy = hist_copy(step, off)
            copy.start()
            hist_copies.append(copy)

    mine = pl.ds(pl.multiple_of(slab * loc, loc), loc)
    table = pt_ref[:, mine, :].reshape(rows, 3)
    weights = wm[:, mine, :].reshape(rows, WMAX)
    for d in range(1, STEPS):
        acc = jnp.zeros((rows, 1), F32)
        for j in range(min(WMAX, d)):
            acc = jnp.where(table[:, 1:2] == d - j, weights[:, j : j + 1], acc)
        recent_w[d] = jnp.broadcast_to(acc, (rows, src))
    target = lax.broadcasted_iota(jnp.int32, (rows, total), 1)
    onehot[...] = (target == table[:, 0:1]).astype(F32).T.astype(BF16)
    for step in range(STEPS):
        inc[step] = inc_ref[:, step, :]

    def repeat(a):
        return jnp.broadcast_to(a[:, None, :], (patches, loc, src)).reshape(rows, src)

    def prepare(step):
        for off in range(1, n_slab):
            hist_copies[step * (n_slab - 1) + off - 1].wait_recv()
        acc = hsend[step, slab].astype(F32)
        for off in range(1, n_slab):
            acc = acc + hrecv[step, off].astype(F32)
        for d in range(2, step + 1):
            acc = acc + recent_w[d] * repeat(amps[step - d])
        pre[...] = acc

    prepare(0)
    for load in loads:
        load.wait()

    remote = []
    for step in range(STEPS):
        driven = pre[...]
        if step > 0:
            driven = driven + recent_w[1] * repeat(amps[step - 1])
        pre[...] = driven

        def couple(p, carry):
            at = pl.ds(pl.multiple_of(p * loc, loc), loc)
            coupled[at, :] = own_blocks(pre[at, :], coup[p])
            return carry

        lax.fori_loop(0, patches, couple, 0, unroll=True)
        whole = coupled[...]
        high = whole.astype(BF16)
        low = (whole - high.astype(F32)).astype(BF16)
        field = jnp.dot(onehot[...], high, preferred_element_type=F32) + jnp.dot(
            onehot[...], low, preferred_element_type=F32
        )
        fsend[step] = field.astype(BF16).reshape(n_patch, patches, src)
        copies = [field_copy(step, off) for off in range(1, n_patch)]
        for copy in copies:
            copy.start()
        for copy in copies:
            copy.wait_recv()
        remote += copies
        share = fsend[step, me].astype(F32)
        for off in range(1, n_patch):
            share = share + frecv[step, off].astype(F32)
        zbuf[step, 0] = share.astype(BF16)
        copies = [slab_copy(step, off) for off in range(1, n_slab)]
        for copy in copies:
            copy.start()
        if step + 1 < STEPS:
            prepare(step + 1)
        for copy in copies:
            copy.wait_recv()
        remote += copies
        scattered = zbuf[step, lax.rem(slab, n_slab)].astype(F32)
        for t in range(1, n_slab):
            scattered = scattered + zbuf[step, lax.rem(slab + n_slab - t, n_slab)].astype(F32)
        drive = inc[step] - scattered
        half = inv.shape[1] // src
        amp = jnp.concatenate(
            [own_blocks(drive[g * half : (g + 1) * half], inv[g]) for g in range(patches // half)],
            axis=0,
        ).astype(BF16)
        out_ref[step] = amp
        amps[step] = amp.astype(F32)

    for copy in hist_copies:
        copy.wait_send()
    for copy in remote:
        copy.wait_send()


def on_device(n_patch, n_slab, history, interp_weights, pair_table, coupling, self_inverse, incident):
    patches, slab_len, src = history.shape
    pairs = pair_table.shape[1]
    loc = coupling.shape[1]
    rows = patches * loc
    total = n_patch * patches
    group = 8
    vmem = pl.BlockSpec(memory_space=pltpu.VMEM)
    hbm = pl.BlockSpec(memory_space=pl.ANY)
    dma = pltpu.SemaphoreType.DMA
    out = pl.pallas_call(
        functools.partial(march, n_patch, n_slab),
        out_shape=jax.ShapeDtypeStruct((STEPS, patches, src), BF16),
        in_specs=[vmem, vmem, vmem, hbm, hbm, vmem],
        out_specs=vmem,
        scratch_shapes=[
            pltpu.VMEM((patches, loc * src, src), BF16),
            pltpu.VMEM((patches // group, group * src, src), BF16),
            pltpu.VMEM((patches, pairs, WMAX), F32),
            pltpu.VMEM((STEPS, rows, src), F32),
            pltpu.VMEM((total, rows), BF16),
            pltpu.VMEM((STEPS, patches, src), F32),
            pltpu.VMEM((STEPS, patches, src), F32),
            pltpu.VMEM((rows, src), F32),
            pltpu.VMEM((rows, src), F32),
            pltpu.VMEM((STEPS, n_slab, rows, src), BF16),
            pltpu.VMEM((STEPS, n_slab, rows, src), BF16),
            pltpu.VMEM((STEPS, n_patch, patches, src), BF16),
            pltpu.VMEM((STEPS, n_patch, patches, src), BF16),
            pltpu.VMEM((STEPS, n_slab, patches, src), BF16),
            dma((5,)),
            dma((STEPS, n_slab)),
            dma((STEPS, n_slab)),
            dma((STEPS, n_patch)),
            dma((STEPS, n_patch)),
            dma((STEPS, n_slab)),
            dma((STEPS, n_slab)),
        ],
        compiler_params=pltpu.CompilerParams(
            collective_id=0, has_side_effects=True, vmem_limit_bytes=40 * 1024 * 1024
        ),
    )(
        history,
        interp_weights,
        pair_table,
        coupling.reshape(patches, loc * src, src),
        self_inverse.reshape(patches // group, group * src, src),
        incident,
    )
    return out.transpose(1, 0, 2)


def solution(mesh):
    in_specs = (
        P("patch", "slab", None),
        P("patch", None, None),
        P("patch", None, None),
        P("patch", "slab", None, None),
        P("patch", None, None),
        P("patch", None, None),
    )
    out_specs = P("patch", None, None)
    return jax.shard_map(
        functools.partial(on_device, mesh.shape["patch"], mesh.shape["slab"]),
        mesh=mesh,
        in_specs=in_specs,
        out_specs=out_specs,
        check_vma=False,
    )
```

```python
import functools

import jax
import jax.numpy as jnp
from jax import lax
from jax.experimental import pallas as pl
from jax.experimental.pallas import tpu as pltpu
from jax.sharding import PartitionSpec as P

WMAX = 4
STEPS = 4
MESH = pl.DeviceIdType.MESH
F32 = jnp.float32
BF16 = jnp.bfloat16


def nt_dot(x, m):
    return lax.dot_general(x, m, (((1,), (1,)), ((), ())), preferred_element_type=F32)


def own_blocks(x, m):
    rows, src = x.shape
    full = nt_dot(x.astype(BF16), m)
    row = lax.broadcasted_iota(jnp.int32, (rows, src), 0)
    out = full[:, :src]
    for r in range(1, rows):
        out = jnp.where(row == r, full[:, r * src : (r + 1) * src], out)
    return out


def march(
    n_patch,
    n_slab,
    hist_hbm,
    w_hbm,
    pt_hbm,
    coup_hbm,
    inv_hbm,
    inc_hbm,
    out_ref,
    hist_ref,
    w_ref,
    pt_ref,
    inc_ref,
    coup,
    inv,
    first_t,
    obs_t,
    wm,
    recent_w,
    onehot,
    inc,
    amps,
    pre,
    coupled,
    hsend,
    hrecv,
    fsend,
    frecv,
    zbuf,
    local_sem,
    h_send_sem,
    h_recv_sem,
    f_send_sem,
    f_recv_sem,
    z_send_sem,
    z_recv_sem,
):
    patches, slab_len, src = hist_ref.shape
    pairs = pt_ref.shape[2]
    loc = pairs // n_slab
    rows = patches * loc
    total = n_patch * patches
    me = lax.axis_index("patch")
    slab = lax.axis_index("slab")

    def patch_peer(off):
        return lax.rem(me + off, n_patch)

    def slab_peer(off):
        return lax.rem(slab + off, n_slab)

    small = [(pt_hbm, pt_ref), (w_hbm, w_ref), (hist_hbm, hist_ref), (inc_hbm, inc_ref)]
    small = [
        pltpu.make_async_copy(src_hbm, dst, local_sem.at[c])
        for c, (src_hbm, dst) in enumerate(small)
    ]
    for load in small:
        load.start()

    barrier = pltpu.get_barrier_semaphore()
    for off in range(1, n_patch):
        pl.semaphore_signal(
            barrier, inc=1, device_id={"patch": patch_peer(off), "slab": slab}, device_id_type=MESH
        )
    for off in range(1, n_slab):
        pl.semaphore_signal(
            barrier, inc=1, device_id={"patch": me, "slab": slab_peer(off)}, device_id_type=MESH
        )

    parts = 4
    size = patches // parts
    loads = [
        pltpu.make_async_copy(
            coup_hbm.at[pl.ds(c * size, size)],
            coup.at[pl.ds(c * size, size)],
            local_sem.at[len(small) + c],
        )
        for c in range(parts)
    ]
    loads.append(pltpu.make_async_copy(inv_hbm, inv, local_sem.at[len(small) + parts]))
    for load in loads:
        load.start()

    lane = lax.broadcasted_iota(jnp.int32, (pairs, slab_len), 1) + (slab * slab_len + 1)

    def stored_share(p, steps):
        shift = lane - first_t[:, p : p + 1]
        taps = [wm[j, :, p : p + 1] for j in range(WMAX)]
        hits = []
        for step in steps:
            hit = jnp.zeros((pairs, slab_len), F32)
            for j in range(WMAX):
                hit = jnp.where(shift == j - step, taps[j], hit)
            hits.append(hit)
        hit = hits[0] if len(hits) == 1 else jnp.concatenate(hits, axis=0)
        return jnp.dot(hit.astype(BF16), hist_ref[p], preferred_element_type=F32)

    def share_of_steps(steps):
        for i in range(0, patches, 2):
            a = stored_share(i, steps)
            b = stored_share(i + 1, steps)
            for k, step in enumerate(steps):
                for d in range(n_slab):
                    r = k * pairs + d * loc
                    both = jnp.concatenate([a[r : r + loc], b[r : r + loc]], axis=0)
                    hsend[step, d, i * loc : (i + 2) * loc, :] = both.astype(BF16)

    def hist_copy(step, off):
        dest = slab_peer(off)
        return pltpu.make_async_remote_copy(
            src_ref=hsend.at[step, dest],
            dst_ref=hrecv.at[step, off],
            send_sem=h_send_sem.at[step, off],
            recv_sem=h_recv_sem.at[step, off],
            device_id={"patch": me, "slab": dest},
            device_id_type=MESH,
        )

    def field_copy(step, off):
        dest = patch_peer(off)
        return pltpu.make_async_remote_copy(
            src_ref=fsend.at[step, dest],
            dst_ref=frecv.at[step, off],
            send_sem=f_send_sem.at[step, off],
            recv_sem=f_recv_sem.at[step, off],
            device_id={"patch": dest, "slab": slab},
            device_id_type=MESH,
        )

    def slab_copy(step, off):
        return pltpu.make_async_remote_copy(
            src_ref=zbuf.at[step, 0],
            dst_ref=zbuf.at[step, off],
            send_sem=z_send_sem.at[step, off],
            recv_sem=z_recv_sem.at[step, off],
            device_id={"patch": me, "slab": slab_peer(off)},
            device_id_type=MESH,
        )

    small[0].wait()
    small[1].wait()
    obs_t[...] = pt_ref[0].T
    first_t[...] = pt_ref[1].T
    band_t = pt_ref[2].T
    weights = w_ref[...].astype(F32)
    for j in range(WMAX):
        wm[j] = jnp.where(j < band_t, weights[:, j, :].T, 0.0)
    small[2].wait()
    small[3].wait()
    share_of_steps([0])

    pl.semaphore_wait(barrier, n_patch + n_slab - 2)
    hist_copies = []

    def send_hist(step):
        for off in range(1, n_slab):
            copy = hist_copy(step, off)
            copy.start()
            hist_copies.append(copy)

    send_hist(0)
    share_of_steps(list(range(1, STEPS)))
    send_hist(1)

    mine = pl.ds(pl.multiple_of(slab * loc, loc), loc)

    def column(x):
        return jnp.concatenate([x[:, p : p + 1] for p in range(patches)], axis=0)

    first = column(first_t[mine, :])
    taps = [column(wm[j, mine, :]) for j in range(min(WMAX, STEPS - 1))]
    for d in range(1, STEPS):
        acc = jnp.zeros((rows, 1), F32)
        for j in range(min(WMAX, d)):
            acc = jnp.where(first == d - j, taps[j], acc)
        recent_w[d] = jnp.broadcast_to(acc, (rows, src))
    target = lax.broadcasted_iota(jnp.int32, (rows, total), 1)
    onehot[...] = (target == column(obs_t[mine, :])).astype(F32).T.astype(BF16)
    for step in range(STEPS):
        inc[step] = inc_ref[:, step, :]

    def repeat(a):
        return jnp.broadcast_to(a[:, None, :], (patches, loc, src)).reshape(rows, src)

    def prepare(step):
        for off in range(1, n_slab):
            hist_copies[step * (n_slab - 1) + off - 1].wait_recv()
        acc = hsend[step, slab].astype(F32)
        for off in range(1, n_slab):
            acc = acc + hrecv[step, off].astype(F32)
        for d in range(2, step + 1):
            acc = acc + recent_w[d] * repeat(amps[step - d])
        pre[...] = acc

    prepare(0)
    for load in loads:
        load.wait()

    remote = []
    for step in range(STEPS):
        driven = pre[...]
        if step > 0:
            driven = driven + recent_w[1] * repeat(amps[step - 1])
        pre[...] = driven

        def couple(p, carry):
            at = pl.ds(pl.multiple_of(p * loc, loc), loc)
            coupled[at, :] = own_blocks(pre[at, :], coup[p])
            return carry

        lax.fori_loop(0, patches, couple, 0, unroll=True)
        whole = coupled[...]
        high = whole.astype(BF16)
        low = (whole - high.astype(F32)).astype(BF16)
        field = jnp.dot(onehot[...], high, preferred_element_type=F32) + jnp.dot(
            onehot[...], low, preferred_element_type=F32
        )
        fsend[step] = field.astype(BF16).reshape(n_patch, patches, src)
        copies = [field_copy(step, off) for off in range(1, n_patch)]
        for copy in copies:
            copy.start()
        for copy in copies:
            copy.wait_recv()
        remote += copies
        share = fsend[step, me].astype(F32)
        for off in range(1, n_patch):
            share = share + frecv[step, off].astype(F32)
        zbuf[step, 0] = share.astype(BF16)
        copies = [slab_copy(step, off) for off in range(1, n_slab)]
        for copy in copies:
            copy.start()
        if step + 1 < STEPS:
            prepare(step + 1)
        for copy in copies:
            copy.wait_recv()
        remote += copies
        if step + 2 < STEPS:
            send_hist(step + 2)
        scattered = zbuf[step, lax.rem(slab, n_slab)].astype(F32)
        for t in range(1, n_slab):
            scattered = scattered + zbuf[step, lax.rem(slab + n_slab - t, n_slab)].astype(F32)
        drive = inc[step] - scattered
        half = inv.shape[1] // src
        amp = jnp.concatenate(
            [own_blocks(drive[g * half : (g + 1) * half], inv[g]) for g in range(patches // half)],
            axis=0,
        ).astype(BF16)
        out_ref[step] = amp
        amps[step] = amp.astype(F32)

    for copy in hist_copies:
        copy.wait_send()
    for copy in remote:
        copy.wait_send()


def on_device(n_patch, n_slab, history, interp_weights, pair_table, coupling, self_inverse, incident):
    patches, slab_len, src = history.shape
    pairs = pair_table.shape[1]
    loc = coupling.shape[1]
    rows = patches * loc
    total = n_patch * patches
    group = 8
    vmem = pl.BlockSpec(memory_space=pltpu.VMEM)
    hbm = pl.BlockSpec(memory_space=pltpu.HBM)
    dma = pltpu.SemaphoreType.DMA
    out = pl.pallas_call(
        functools.partial(march, n_patch, n_slab),
        out_shape=jax.ShapeDtypeStruct((STEPS, patches, src), BF16),
        in_specs=[hbm] * 6,
        out_specs=vmem,
        scratch_shapes=[
            pltpu.VMEM((patches, slab_len, src), BF16),
            pltpu.VMEM((patches, WMAX, pairs), BF16),
            pltpu.VMEM((3, patches, pairs), jnp.int32),
            pltpu.VMEM((patches, STEPS, src), F32),
            pltpu.VMEM((patches, loc * src, src), BF16),
            pltpu.VMEM((patches // group, group * src, src), BF16),
            pltpu.VMEM((pairs, patches), jnp.int32),
            pltpu.VMEM((pairs, patches), jnp.int32),
            pltpu.VMEM((WMAX, pairs, patches), F32),
            pltpu.VMEM((STEPS, rows, src), F32),
            pltpu.VMEM((total, rows), BF16),
            pltpu.VMEM((STEPS, patches, src), F32),
            pltpu.VMEM((STEPS, patches, src), F32),
            pltpu.VMEM((rows, src), F32),
            pltpu.VMEM((rows, src), F32),
            pltpu.VMEM((STEPS, n_slab, rows, src), BF16),
            pltpu.VMEM((STEPS, n_slab, rows, src), BF16),
            pltpu.VMEM((STEPS, n_patch, patches, src), BF16),
            pltpu.VMEM((STEPS, n_patch, patches, src), BF16),
            pltpu.VMEM((STEPS, n_slab, patches, src), BF16),
            dma((9,)),
            dma((STEPS, n_slab)),
            dma((STEPS, n_slab)),
            dma((STEPS, n_patch)),
            dma((STEPS, n_patch)),
            dma((STEPS, n_slab)),
            dma((STEPS, n_slab)),
        ],
        compiler_params=pltpu.CompilerParams(
            collective_id=0, has_side_effects=True, vmem_limit_bytes=63 * 1024 * 1024
        ),
    )(
        history,
        interp_weights.transpose(0, 2, 1),
        pair_table.transpose(2, 0, 1),
        coupling.reshape(patches, loc * src, src),
        self_inverse.reshape(patches // group, group * src, src),
        incident,
    )
    return out.transpose(1, 0, 2)


def solution(mesh):
    in_specs = (
        P("patch", "slab", None),
        P("patch", None, None),
        P("patch", None, None),
        P("patch", "slab", None, None),
        P("patch", None, None),
        P("patch", None, None),
    )
    out_specs = P("patch", None, None)
    return jax.shard_map(
        functools.partial(on_device, mesh.shape["patch"], mesh.shape["slab"]),
        mesh=mesh,
        in_specs=in_specs,
        out_specs=out_specs,
        check_vma=False,
    )
```

```python
import functools

import jax
import jax.numpy as jnp
from jax import lax
from jax.experimental import pallas as pl
from jax.experimental.pallas import tpu as pltpu
from jax.sharding import PartitionSpec as P

WMAX = 4
STEPS = 4
MESH = pl.DeviceIdType.MESH
F32 = jnp.float32
BF16 = jnp.bfloat16


def own_blocks(x, m):
    rows, src = x.shape
    half = rows // 2
    wide = jnp.concatenate([x, x], axis=1)
    row = lax.broadcasted_iota(jnp.int32, wide.shape, 0)
    lane = lax.broadcasted_iota(jnp.int32, wide.shape, 1)
    wide = jnp.where((row < half) == (lane < src), wide, 0.0).astype(BF16)
    full = jnp.dot(wide, m, preferred_element_type=F32)
    row = lax.rem(lax.broadcasted_iota(jnp.int32, (rows, src), 0), half)
    out = full[:, :src]
    for r in range(1, half):
        out = jnp.where(row == r, full[:, r * src : (r + 1) * src], out)
    return out


def march(
    n_patch,
    n_slab,
    hist_hbm,
    w_hbm,
    pt_hbm,
    coup_hbm,
    inv_hbm,
    inc_hbm,
    out_ref,
    hist_ref,
    w_ref,
    pt_ref,
    inc_ref,
    coup,
    inv,
    coup_t,
    inv_t,
    first_t,
    obs_t,
    wm,
    recent_w,
    onehot,
    inc,
    amps,
    pre,
    coupled,
    hsend,
    hrecv,
    fsend,
    frecv,
    zbuf,
    local_sem,
    h_send_sem,
    h_recv_sem,
    f_send_sem,
    f_recv_sem,
    z_send_sem,
    z_recv_sem,
):
    patches, slab_len, src = hist_ref.shape
    pairs = pt_ref.shape[2]
    loc = pairs // n_slab
    rows = patches * loc
    total = n_patch * patches
    me = lax.axis_index("patch")
    slab = lax.axis_index("slab")

    def patch_peer(off):
        return lax.rem(me + off, n_patch)

    def slab_peer(off):
        return lax.rem(slab + off, n_slab)

    small = [(pt_hbm, pt_ref), (w_hbm, w_ref), (hist_hbm, hist_ref), (inc_hbm, inc_ref)]
    small = [
        pltpu.make_async_copy(src_hbm, dst, local_sem.at[c])
        for c, (src_hbm, dst) in enumerate(small)
    ]
    for load in small:
        load.start()

    barrier = pltpu.get_barrier_semaphore()
    for off in range(1, n_patch):
        pl.semaphore_signal(
            barrier, inc=1, device_id={"patch": patch_peer(off), "slab": slab}, device_id_type=MESH
        )
    for off in range(1, n_slab):
        pl.semaphore_signal(
            barrier, inc=1, device_id={"patch": me, "slab": slab_peer(off)}, device_id_type=MESH
        )

    parts = 4
    size = patches // parts
    loads = [
        pltpu.make_async_copy(
            coup_hbm.at[pl.ds(c * size, size)],
            coup.at[pl.ds(c * size, size)],
            local_sem.at[len(small) + c],
        )
        for c in range(parts)
    ]
    loads.append(pltpu.make_async_copy(inv_hbm, inv, local_sem.at[len(small) + parts]))
    for load in loads:
        load.start()

    lane = lax.broadcasted_iota(jnp.int32, (pairs, slab_len), 1) + (slab * slab_len + 1)

    def stored_share(p, steps):
        shift = lane - first_t[:, p : p + 1]
        taps = [wm[j, :, p : p + 1] for j in range(WMAX)]
        hits = []
        for step in steps:
            hit = jnp.zeros((pairs, slab_len), F32)
            for j in range(WMAX):
                hit = jnp.where(shift == j - step, taps[j], hit)
            hits.append(hit)
        hit = hits[0] if len(hits) == 1 else jnp.concatenate(hits, axis=0)
        return jnp.dot(hit.astype(BF16), hist_ref[p], preferred_element_type=F32)

    def share_of_steps(steps):
        for i in range(0, patches, 2):
            a = stored_share(i, steps)
            b = stored_share(i + 1, steps)
            for k, step in enumerate(steps):
                for d in range(n_slab):
                    r = k * pairs + d * loc
                    both = jnp.concatenate([a[r : r + loc], b[r : r + loc]], axis=0)
                    hsend[step, d, i * loc : (i + 2) * loc, :] = both.astype(BF16)

    def hist_copy(step, off):
        dest = slab_peer(off)
        return pltpu.make_async_remote_copy(
            src_ref=hsend.at[step, dest],
            dst_ref=hrecv.at[step, off],
            send_sem=h_send_sem.at[step, off],
            recv_sem=h_recv_sem.at[step, off],
            device_id={"patch": me, "slab": dest},
            device_id_type=MESH,
        )

    def field_copy(step, off):
        dest = patch_peer(off)
        return pltpu.make_async_remote_copy(
            src_ref=fsend.at[step, dest],
            dst_ref=frecv.at[step, off],
            send_sem=f_send_sem.at[step, off],
            recv_sem=f_recv_sem.at[step, off],
            device_id={"patch": dest, "slab": slab},
            device_id_type=MESH,
        )

    def slab_copy(step, off):
        return pltpu.make_async_remote_copy(
            src_ref=zbuf.at[step, 0],
            dst_ref=zbuf.at[step, off],
            send_sem=z_send_sem.at[step, off],
            recv_sem=z_recv_sem.at[step, off],
            device_id={"patch": me, "slab": slab_peer(off)},
            device_id_type=MESH,
        )

    small[0].wait()
    small[1].wait()
    obs_t[...] = pt_ref[0].T
    first_t[...] = pt_ref[1].T
    band_t = pt_ref[2].T
    weights = w_ref[...].astype(F32)
    for j in range(WMAX):
        wm[j] = jnp.where(j < band_t, weights[:, j, :].T, 0.0)
    small[2].wait()
    small[3].wait()
    share_of_steps([0])

    pl.semaphore_wait(barrier, n_patch + n_slab - 2)
    hist_copies = []

    def send_hist(step):
        for off in range(1, n_slab):
            copy = hist_copy(step, off)
            copy.start()
            hist_copies.append(copy)

    send_hist(0)
    share_of_steps(list(range(1, STEPS)))
    send_hist(1)

    mine = pl.ds(pl.multiple_of(slab * loc, loc), loc)

    def column(x):
        return jnp.concatenate([x[:, p : p + 1] for p in range(patches)], axis=0)

    first = column(first_t[mine, :])
    taps = [column(wm[j, mine, :]) for j in range(min(WMAX, STEPS - 1))]
    for d in range(1, STEPS):
        acc = jnp.zeros((rows, 1), F32)
        for j in range(min(WMAX, d)):
            acc = jnp.where(first == d - j, taps[j], acc)
        recent_w[d] = jnp.broadcast_to(acc, (rows, src))
    target = lax.broadcasted_iota(jnp.int32, (rows, total), 1)
    onehot[...] = (target == column(obs_t[mine, :])).astype(F32).T.astype(BF16)
    for step in range(STEPS):
        inc[step] = inc_ref[:, step, :]

    def repeat(a):
        return jnp.broadcast_to(a[:, None, :], (patches, loc, src)).reshape(rows, src)

    def prepare(step):
        for off in range(1, n_slab):
            hist_copies[step * (n_slab - 1) + off - 1].wait_recv()
        acc = hsend[step, slab].astype(F32)
        for off in range(1, n_slab):
            acc = acc + hrecv[step, off].astype(F32)
        for d in range(2, step + 1):
            acc = acc + recent_w[d] * repeat(amps[step - d])
        pre[...] = acc

    for load in loads:
        load.wait()

    def turn(stored, turned):
        pairs_of, _, width = turned.shape
        for g in range(pairs_of):
            for h in range(2):
                for r in range(width // src):
                    block = stored[2 * g + h, r * src : (r + 1) * src, :]
                    turned[g, h * src : (h + 1) * src, r * src : (r + 1) * src] = block.T

    turn(coup, coup_t)
    turn(inv, inv_t)
    prepare(0)

    remote = []
    for step in range(STEPS):
        driven = pre[...]
        if step > 0:
            driven = driven + recent_w[1] * repeat(amps[step - 1])
        pre[...] = driven

        def couple(p, carry):
            at = pl.ds(pl.multiple_of(p * 2 * loc, 2 * loc), 2 * loc)
            coupled[at, :] = own_blocks(pre[at, :], coup_t[p])
            return carry

        lax.fori_loop(0, patches // 2, couple, 0, unroll=True)
        whole = coupled[...]
        high = whole.astype(BF16)
        low = (whole - high.astype(F32)).astype(BF16)
        field = jnp.dot(onehot[...], high, preferred_element_type=F32) + jnp.dot(
            onehot[...], low, preferred_element_type=F32
        )
        fsend[step] = field.astype(BF16).reshape(n_patch, patches, src)
        copies = [field_copy(step, off) for off in range(1, n_patch)]
        for copy in copies:
            copy.start()
        for copy in copies:
            copy.wait_recv()
        remote += copies
        share = fsend[step, me].astype(F32)
        for off in range(1, n_patch):
            share = share + frecv[step, off].astype(F32)
        zbuf[step, 0] = share.astype(BF16)
        copies = [slab_copy(step, off) for off in range(1, n_slab)]
        for copy in copies:
            copy.start()
        if step + 1 < STEPS:
            prepare(step + 1)
        for copy in copies:
            copy.wait_recv()
        remote += copies
        if step + 2 < STEPS:
            send_hist(step + 2)
        scattered = zbuf[step, lax.rem(slab, n_slab)].astype(F32)
        for t in range(1, n_slab):
            scattered = scattered + zbuf[step, lax.rem(slab + n_slab - t, n_slab)].astype(F32)
        drive = inc[step] - scattered
        amp = own_blocks(drive, inv_t[0]).astype(BF16)
        out_ref[step] = amp
        amps[step] = amp.astype(F32)

    for copy in hist_copies:
        copy.wait_send()
    for copy in remote:
        copy.wait_send()


def on_device(n_patch, n_slab, history, interp_weights, pair_table, coupling, self_inverse, incident):
    patches, slab_len, src = history.shape
    pairs = pair_table.shape[1]
    loc = coupling.shape[1]
    rows = patches * loc
    total = n_patch * patches
    group = patches // 2
    vmem = pl.BlockSpec(memory_space=pltpu.VMEM)
    hbm = pl.BlockSpec(memory_space=pltpu.HBM)
    dma = pltpu.SemaphoreType.DMA
    out = pl.pallas_call(
        functools.partial(march, n_patch, n_slab),
        out_shape=jax.ShapeDtypeStruct((STEPS, patches, src), BF16),
        in_specs=[hbm] * 6,
        out_specs=vmem,
        scratch_shapes=[
            pltpu.VMEM((patches, slab_len, src), BF16),
            pltpu.VMEM((patches, WMAX, pairs), BF16),
            pltpu.VMEM((3, patches, pairs), jnp.int32),
            pltpu.VMEM((patches, STEPS, src), F32),
            pltpu.VMEM((patches, loc * src, src), BF16),
            pltpu.VMEM((patches // group, group * src, src), BF16),
            pltpu.VMEM((patches // 2, 2 * src, loc * src), BF16),
            pltpu.VMEM((1, 2 * src, group * src), BF16),
            pltpu.VMEM((pairs, patches), jnp.int32),
            pltpu.VMEM((pairs, patches), jnp.int32),
            pltpu.VMEM((WMAX, pairs, patches), F32),
            pltpu.VMEM((STEPS, rows, src), F32),
            pltpu.VMEM((total, rows), BF16),
            pltpu.VMEM((STEPS, patches, src), F32),
            pltpu.VMEM((STEPS, patches, src), F32),
            pltpu.VMEM((rows, src), F32),
            pltpu.VMEM((rows, src), F32),
            pltpu.VMEM((STEPS, n_slab, rows, src), BF16),
            pltpu.VMEM((STEPS, n_slab, rows, src), BF16),
            pltpu.VMEM((STEPS, n_patch, patches, src), BF16),
            pltpu.VMEM((STEPS, n_patch, patches, src), BF16),
            pltpu.VMEM((STEPS, n_slab, patches, src), BF16),
            dma((9,)),
            dma((STEPS, n_slab)),
            dma((STEPS, n_slab)),
            dma((STEPS, n_patch)),
            dma((STEPS, n_patch)),
            dma((STEPS, n_slab)),
            dma((STEPS, n_slab)),
        ],
        compiler_params=pltpu.CompilerParams(
            collective_id=0, has_side_effects=True, vmem_limit_bytes=63 * 1024 * 1024
        ),
    )(
        history,
        interp_weights.transpose(0, 2, 1),
        pair_table.transpose(2, 0, 1),
        coupling.reshape(patches, loc * src, src),
        self_inverse.reshape(patches // group, group * src, src),
        incident,
    )
    return out.transpose(1, 0, 2)


def solution(mesh):
    in_specs = (
        P("patch", "slab", None),
        P("patch", None, None),
        P("patch", None, None),
        P("patch", "slab", None, None),
        P("patch", None, None),
        P("patch", None, None),
    )
    out_specs = P("patch", None, None)
    return jax.shard_map(
        functools.partial(on_device, mesh.shape["patch"], mesh.shape["slab"]),
        mesh=mesh,
        in_specs=in_specs,
        out_specs=out_specs,
        check_vma=False,
    )
```

```python
import functools

import jax
import jax.numpy as jnp
from jax import lax
from jax.experimental import pallas as pl
from jax.experimental.pallas import tpu as pltpu
from jax.sharding import PartitionSpec as P

WMAX = 4
STEPS = 4
MESH = pl.DeviceIdType.MESH
F32 = jnp.float32
BF16 = jnp.bfloat16


def own_blocks(x, m):
    rows, src = x.shape
    half = rows // 2
    wide = jnp.concatenate([x, x], axis=1)
    row = lax.broadcasted_iota(jnp.int32, wide.shape, 0)
    lane = lax.broadcasted_iota(jnp.int32, wide.shape, 1)
    wide = jnp.where((row < half) == (lane < src), wide, 0.0).astype(BF16)
    full = jnp.dot(wide, m, preferred_element_type=F32)
    row = lax.rem(lax.broadcasted_iota(jnp.int32, (rows, src), 0), half)
    out = full[:, :src]
    for r in range(1, half):
        out = jnp.where(row == r, full[:, r * src : (r + 1) * src], out)
    return out


def march(
    n_patch,
    n_slab,
    hist_hbm,
    w_hbm,
    pt_hbm,
    coup_hbm,
    inv_hbm,
    inc_hbm,
    out_ref,
    hist_ref,
    w_ref,
    pt_ref,
    inc_ref,
    coup,
    inv,
    coup_t,
    inv_t,
    first_t,
    obs_t,
    wm,
    recent_w,
    onehot,
    inc,
    amps,
    pre,
    coupled,
    hsend,
    hrecv,
    fsend,
    frecv,
    zbuf,
    local_sem,
    h_send_sem,
    h_recv_sem,
    f_send_sem,
    f_recv_sem,
    z_send_sem,
    z_recv_sem,
):
    patches, slab_len, src = hist_ref.shape
    pairs = pt_ref.shape[2]
    loc = pairs // n_slab
    rows = patches * loc
    total = n_patch * patches
    me = lax.axis_index("patch")
    slab = lax.axis_index("slab")

    def patch_peer(off):
        return lax.rem(me + off, n_patch)

    def slab_peer(off):
        return lax.rem(slab + off, n_slab)

    small = [(pt_hbm, pt_ref), (w_hbm, w_ref), (hist_hbm, hist_ref), (inc_hbm, inc_ref)]
    small = [
        pltpu.make_async_copy(src_hbm, dst, local_sem.at[c])
        for c, (src_hbm, dst) in enumerate(small)
    ]
    for load in small:
        load.start()

    barrier = pltpu.get_barrier_semaphore()
    for off in range(1, n_patch):
        pl.semaphore_signal(
            barrier, inc=1, device_id={"patch": patch_peer(off), "slab": slab}, device_id_type=MESH
        )
    for off in range(1, n_slab):
        pl.semaphore_signal(
            barrier, inc=1, device_id={"patch": me, "slab": slab_peer(off)}, device_id_type=MESH
        )

    parts = 4
    size = patches // parts
    loads = [
        pltpu.make_async_copy(
            coup_hbm.at[pl.ds(c * size, size)],
            coup.at[pl.ds(c * size, size)],
            local_sem.at[len(small) + c],
        )
        for c in range(parts)
    ]
    loads.append(pltpu.make_async_copy(inv_hbm, inv, local_sem.at[len(small) + parts]))
    for load in loads:
        load.start()

    lane = lax.broadcasted_iota(jnp.int32, (pairs, slab_len), 1) + (slab * slab_len + 1)

    def stored_share(p, steps):
        shift = lane - first_t[:, p : p + 1]
        taps = [wm[j, :, p : p + 1] for j in range(WMAX)]
        hits = []
        for step in steps:
            hit = jnp.zeros((pairs, slab_len), F32)
            for j in range(WMAX):
                hit = jnp.where(shift == j - step, taps[j], hit)
            hits.append(hit)
        hit = hits[0] if len(hits) == 1 else jnp.concatenate(hits, axis=0)
        return jnp.dot(hit.astype(BF16), hist_ref[p], preferred_element_type=F32)

    def share_of_steps(steps):
        for i in range(0, patches, 2):
            a = stored_share(i, steps)
            b = stored_share(i + 1, steps)
            for k, step in enumerate(steps):
                for d in range(n_slab):
                    r = k * pairs + d * loc
                    both = jnp.concatenate([a[r : r + loc], b[r : r + loc]], axis=0)
                    hsend[step, d, i * loc : (i + 2) * loc, :] = both.astype(BF16)

    def hist_copy(step, off):
        dest = slab_peer(off)
        return pltpu.make_async_remote_copy(
            src_ref=hsend.at[step, dest],
            dst_ref=hrecv.at[step, off],
            send_sem=h_send_sem.at[step],
            recv_sem=h_recv_sem.at[step],
            device_id={"patch": me, "slab": dest},
            device_id_type=MESH,
        )

    def field_copy(step, off):
        dest = patch_peer(off)
        return pltpu.make_async_remote_copy(
            src_ref=fsend.at[step, dest],
            dst_ref=frecv.at[step, off],
            send_sem=f_send_sem.at[step],
            recv_sem=f_recv_sem.at[step],
            device_id={"patch": dest, "slab": slab},
            device_id_type=MESH,
        )

    def slab_copy(step, off):
        return pltpu.make_async_remote_copy(
            src_ref=zbuf.at[step, 0],
            dst_ref=zbuf.at[step, off],
            send_sem=z_send_sem.at[step],
            recv_sem=z_recv_sem.at[step],
            device_id={"patch": me, "slab": slab_peer(off)},
            device_id_type=MESH,
        )

    def all_of(step, ref, send_sem, recv_sem):
        slots = ref.at[step, pl.ds(1, ref.shape[1] - 1)]
        return pltpu.make_async_remote_copy(
            src_ref=slots,
            dst_ref=slots,
            send_sem=send_sem.at[step],
            recv_sem=recv_sem.at[step],
            device_id={"patch": me, "slab": slab_peer(1)},
            device_id_type=MESH,
        )

    small[0].wait()
    small[1].wait()
    obs_t[...] = pt_ref[0].T
    first_t[...] = pt_ref[1].T
    band_t = pt_ref[2].T
    weights = w_ref[...].astype(F32)
    for j in range(WMAX):
        wm[j] = jnp.where(j < band_t, weights[:, j, :].T, 0.0)
    small[2].wait()
    small[3].wait()
    share_of_steps([0])

    pl.semaphore_wait(barrier, n_patch + n_slab - 2)

    def send_hist(step):
        for off in range(n_slab - 1, 0, -1):
            hist_copy(step, off).start()

    send_hist(0)
    share_of_steps([1])
    send_hist(1)

    mine = pl.ds(pl.multiple_of(slab * loc, loc), loc)

    def column(x):
        return jnp.concatenate([x[:, p : p + 1] for p in range(patches)], axis=0)

    first = column(first_t[mine, :])
    taps = [column(wm[j, mine, :]) for j in range(min(WMAX, STEPS - 1))]
    for d in range(1, STEPS):
        acc = jnp.zeros((rows, 1), F32)
        for j in range(min(WMAX, d)):
            acc = jnp.where(first == d - j, taps[j], acc)
        recent_w[d] = jnp.broadcast_to(acc, (rows, src))
    target = lax.broadcasted_iota(jnp.int32, (rows, total), 1)
    onehot[...] = (target == column(obs_t[mine, :])).astype(F32).T.astype(BF16)
    for step in range(STEPS):
        inc[step] = inc_ref[:, step, :]

    def repeat(a):
        return jnp.broadcast_to(a[:, None, :], (patches, loc, src)).reshape(rows, src)

    def prepare(step):
        all_of(step, hrecv, h_send_sem, h_recv_sem).wait_recv()
        acc = hsend[step, slab].astype(F32)
        for off in range(1, n_slab):
            acc = acc + hrecv[step, off].astype(F32)
        for d in range(2, step + 1):
            acc = acc + recent_w[d] * repeat(amps[step - d])
        pre[...] = acc

    for load in loads:
        load.wait()

    def turn(stored, turned):
        pairs_of, _, width = turned.shape
        for g in range(pairs_of):
            for h in range(2):
                for r in range(width // src):
                    block = stored[2 * g + h, r * src : (r + 1) * src, :]
                    turned[g, h * src : (h + 1) * src, r * src : (r + 1) * src] = block.T

    turn(coup, coup_t)
    turn(inv, inv_t)
    prepare(0)

    for step in range(STEPS):
        driven = pre[...]
        if step > 0:
            driven = driven + recent_w[1] * repeat(amps[step - 1])
        pre[...] = driven

        def couple(p, carry):
            at = pl.ds(pl.multiple_of(p * 2 * loc, 2 * loc), 2 * loc)
            coupled[at, :] = own_blocks(pre[at, :], coup_t[p])
            return carry

        lax.fori_loop(0, patches // 2, couple, 0, unroll=True)
        whole = coupled[...]
        high = whole.astype(BF16)
        low = (whole - high.astype(F32)).astype(BF16)
        field = jnp.dot(onehot[...], high, preferred_element_type=F32) + jnp.dot(
            onehot[...], low, preferred_element_type=F32
        )
        fsend[step] = field.astype(BF16).reshape(n_patch, patches, src)
        for off in range(n_patch - 1, 0, -1):
            field_copy(step, off).start()
        if step == 0:
            share_of_steps(list(range(2, STEPS)))
        all_of(step, frecv, f_send_sem, f_recv_sem).wait_recv()
        share = fsend[step, me].astype(F32)
        for off in range(1, n_patch):
            share = share + frecv[step, off].astype(F32)
        zbuf[step, 0] = share.astype(BF16)
        for off in range(n_slab - 1, 0, -1):
            slab_copy(step, off).start()
        if step + 1 < STEPS:
            prepare(step + 1)
        all_of(step, zbuf, z_send_sem, z_recv_sem).wait_recv()
        if step + 2 < STEPS:
            send_hist(step + 2)
        scattered = zbuf[step, lax.rem(slab, n_slab)].astype(F32)
        for t in range(1, n_slab):
            scattered = scattered + zbuf[step, lax.rem(slab + n_slab - t, n_slab)].astype(F32)
        drive = inc[step] - scattered
        amp = own_blocks(drive, inv_t[0]).astype(BF16)
        out_ref[step] = amp
        amps[step] = amp.astype(F32)

    for step in range(STEPS):
        all_of(step, hsend, h_send_sem, h_recv_sem).wait_send()
        all_of(step, fsend, f_send_sem, f_recv_sem).wait_send()
        all_of(step, zbuf, z_send_sem, z_recv_sem).wait_send()


def on_device(n_patch, n_slab, history, interp_weights, pair_table, coupling, self_inverse, incident):
    patches, slab_len, src = history.shape
    pairs = pair_table.shape[1]
    loc = coupling.shape[1]
    rows = patches * loc
    total = n_patch * patches
    group = patches // 2
    vmem = pl.BlockSpec(memory_space=pltpu.VMEM)
    hbm = pl.BlockSpec(memory_space=pltpu.HBM)
    dma = pltpu.SemaphoreType.DMA
    out = pl.pallas_call(
        functools.partial(march, n_patch, n_slab),
        out_shape=jax.ShapeDtypeStruct((STEPS, patches, src), BF16),
        in_specs=[hbm] * 6,
        out_specs=vmem,
        scratch_shapes=[
            pltpu.VMEM((patches, slab_len, src), BF16),
            pltpu.VMEM((patches, WMAX, pairs), BF16),
            pltpu.VMEM((3, patches, pairs), jnp.int32),
            pltpu.VMEM((patches, STEPS, src), F32),
            pltpu.VMEM((patches, loc * src, src), BF16),
            pltpu.VMEM((patches // group, group * src, src), BF16),
            pltpu.VMEM((patches // 2, 2 * src, loc * src), BF16),
            pltpu.VMEM((1, 2 * src, group * src), BF16),
            pltpu.VMEM((pairs, patches), jnp.int32),
            pltpu.VMEM((pairs, patches), jnp.int32),
            pltpu.VMEM((WMAX, pairs, patches), F32),
            pltpu.VMEM((STEPS, rows, src), F32),
            pltpu.VMEM((total, rows), BF16),
            pltpu.VMEM((STEPS, patches, src), F32),
            pltpu.VMEM((STEPS, patches, src), F32),
            pltpu.VMEM((rows, src), F32),
            pltpu.VMEM((rows, src), F32),
            pltpu.VMEM((STEPS, n_slab, rows, src), BF16),
            pltpu.VMEM((STEPS, n_slab, rows, src), BF16),
            pltpu.VMEM((STEPS, n_patch, patches, src), BF16),
            pltpu.VMEM((STEPS, n_patch, patches, src), BF16),
            pltpu.VMEM((STEPS, n_slab, patches, src), BF16),
            dma((9,)),
            dma((STEPS,)),
            dma((STEPS,)),
            dma((STEPS,)),
            dma((STEPS,)),
            dma((STEPS,)),
            dma((STEPS,)),
        ],
        compiler_params=pltpu.CompilerParams(
            collective_id=0, has_side_effects=True, vmem_limit_bytes=63 * 1024 * 1024
        ),
    )(
        history,
        interp_weights.transpose(0, 2, 1),
        pair_table.transpose(2, 0, 1),
        coupling.reshape(patches, loc * src, src),
        self_inverse.reshape(patches // group, group * src, src),
        incident,
    )
    return out.transpose(1, 0, 2)


def solution(mesh):
    in_specs = (
        P("patch", "slab", None),
        P("patch", None, None),
        P("patch", None, None),
        P("patch", "slab", None, None),
        P("patch", None, None),
        P("patch", None, None),
    )
    out_specs = P("patch", None, None)
    return jax.shard_map(
        functools.partial(on_device, mesh.shape["patch"], mesh.shape["slab"]),
        mesh=mesh,
        in_specs=in_specs,
        out_specs=out_specs,
        check_vma=False,
    )
```

```python
import functools

import jax
import jax.numpy as jnp
from jax import lax
from jax.experimental import pallas as pl
from jax.experimental.pallas import tpu as pltpu
from jax.sharding import PartitionSpec as P

WMAX = 4
STEPS = 4
MESH = pl.DeviceIdType.MESH
F32 = jnp.float32
BF16 = jnp.bfloat16


def own_blocks(x, first, second):
    rows, src = x.shape
    half = rows // 2
    wide = jnp.concatenate([x, x], axis=1)
    row = lax.broadcasted_iota(jnp.int32, wide.shape, 0)
    lane = lax.broadcasted_iota(jnp.int32, wide.shape, 1)
    wide = jnp.where((row < half) == (lane < src), wide, 0.0).astype(BF16)
    full = lax.dot_general(
        wide,
        jnp.concatenate([first, second], axis=1),
        (((1,), (1,)), ((), ())),
        preferred_element_type=F32,
    )
    row = lax.rem(lax.broadcasted_iota(jnp.int32, (rows, src), 0), half)
    out = full[:, :src]
    for r in range(1, half):
        out = jnp.where(row == r, full[:, r * src : (r + 1) * src], out)
    return out


def march(
    n_patch,
    n_slab,
    hist_hbm,
    w_hbm,
    pt_hbm,
    coup_hbm,
    inv_hbm,
    inc_hbm,
    out_ref,
    hist_ref,
    w_ref,
    pt_ref,
    inc_ref,
    coup,
    inv,
    first_t,
    obs_t,
    wm,
    recent_w,
    onehot,
    inc,
    amps,
    pre,
    coupled,
    hsend,
    hrecv,
    fsend,
    frecv,
    zbuf,
    local_sem,
    h_send_sem,
    h_recv_sem,
    f_send_sem,
    f_recv_sem,
    z_send_sem,
    z_recv_sem,
):
    patches, slab_len, src = hist_ref.shape
    pairs = pt_ref.shape[2]
    loc = pairs // n_slab
    rows = patches * loc
    total = n_patch * patches
    me = lax.axis_index("patch")
    slab = lax.axis_index("slab")

    def patch_peer(off):
        return lax.rem(me + off, n_patch)

    def slab_peer(off):
        return lax.rem(slab + off, n_slab)

    small = [(pt_hbm, pt_ref), (w_hbm, w_ref), (hist_hbm, hist_ref), (inc_hbm, inc_ref)]
    small = [
        pltpu.make_async_copy(src_hbm, dst, local_sem.at[c])
        for c, (src_hbm, dst) in enumerate(small)
    ]
    for load in small:
        load.start()

    barrier = pltpu.get_barrier_semaphore()
    for off in range(1, n_patch):
        pl.semaphore_signal(
            barrier, inc=1, device_id={"patch": patch_peer(off), "slab": slab}, device_id_type=MESH
        )
    for off in range(1, n_slab):
        pl.semaphore_signal(
            barrier, inc=1, device_id={"patch": me, "slab": slab_peer(off)}, device_id_type=MESH
        )

    parts = 4
    size = patches // parts
    loads = [
        pltpu.make_async_copy(
            coup_hbm.at[pl.ds(c * size, size)],
            coup.at[pl.ds(c * size, size)],
            local_sem.at[len(small) + c],
        )
        for c in range(parts)
    ]
    loads.append(pltpu.make_async_copy(inv_hbm, inv, local_sem.at[len(small) + parts]))
    for load in loads:
        load.start()

    lane = lax.broadcasted_iota(jnp.int32, (pairs, slab_len), 1) + (slab * slab_len + 1)

    def stored_share(p, steps):
        shift = lane - first_t[:, p : p + 1]
        taps = [wm[j, :, p : p + 1] for j in range(WMAX)]
        hits = []
        for step in steps:
            hit = jnp.zeros((pairs, slab_len), F32)
            for j in range(WMAX):
                hit = jnp.where(shift == j - step, taps[j], hit)
            hits.append(hit)
        hit = hits[0] if len(hits) == 1 else jnp.concatenate(hits, axis=0)
        return jnp.dot(hit.astype(BF16), hist_ref[p], preferred_element_type=F32)

    def share_of_steps(steps):
        for i in range(0, patches, 2):
            a = stored_share(i, steps)
            b = stored_share(i + 1, steps)
            for k, step in enumerate(steps):
                for d in range(n_slab):
                    r = k * pairs + d * loc
                    both = jnp.concatenate([a[r : r + loc], b[r : r + loc]], axis=0)
                    hsend[step, d, i * loc : (i + 2) * loc, :] = both.astype(BF16)

    def hist_copy(step, off):
        dest = slab_peer(off)
        return pltpu.make_async_remote_copy(
            src_ref=hsend.at[step, dest],
            dst_ref=hrecv.at[step, off],
            send_sem=h_send_sem.at[step],
            recv_sem=h_recv_sem.at[step],
            device_id={"patch": me, "slab": dest},
            device_id_type=MESH,
        )

    def field_copy(step, off):
        dest = patch_peer(off)
        return pltpu.make_async_remote_copy(
            src_ref=fsend.at[step, dest],
            dst_ref=frecv.at[step, off],
            send_sem=f_send_sem.at[step],
            recv_sem=f_recv_sem.at[step],
            device_id={"patch": dest, "slab": slab},
            device_id_type=MESH,
        )

    def slab_copy(step, off):
        return pltpu.make_async_remote_copy(
            src_ref=zbuf.at[step, 0],
            dst_ref=zbuf.at[step, off],
            send_sem=z_send_sem.at[step],
            recv_sem=z_recv_sem.at[step],
            device_id={"patch": me, "slab": slab_peer(off)},
            device_id_type=MESH,
        )

    def all_of(step, ref, send_sem, recv_sem):
        slots = ref.at[step, pl.ds(1, ref.shape[1] - 1)]
        return pltpu.make_async_remote_copy(
            src_ref=slots,
            dst_ref=slots,
            send_sem=send_sem.at[step],
            recv_sem=recv_sem.at[step],
            device_id={"patch": me, "slab": slab_peer(1)},
            device_id_type=MESH,
        )

    small[0].wait()
    small[1].wait()
    obs_t[...] = pt_ref[0].T
    first_t[...] = pt_ref[1].T
    band_t = pt_ref[2].T
    weights = w_ref[...].astype(F32)
    for j in range(WMAX):
        wm[j] = jnp.where(j < band_t, weights[:, j, :].T, 0.0)
    small[2].wait()
    small[3].wait()
    share_of_steps([0])

    pl.semaphore_wait(barrier, n_patch + n_slab - 2)

    def send_hist(step):
        for off in range(n_slab - 1, 0, -1):
            hist_copy(step, off).start()

    send_hist(0)
    share_of_steps([1])
    send_hist(1)

    mine = pl.ds(pl.multiple_of(slab * loc, loc), loc)

    def column(x):
        return jnp.concatenate([x[:, p : p + 1] for p in range(patches)], axis=0)

    first = column(first_t[mine, :])
    taps = [column(wm[j, mine, :]) for j in range(min(WMAX, STEPS - 1))]
    for d in range(1, STEPS):
        acc = jnp.zeros((rows, 1), F32)
        for j in range(min(WMAX, d)):
            acc = jnp.where(first == d - j, taps[j], acc)
        recent_w[d] = jnp.broadcast_to(acc, (rows, src))
    target = lax.broadcasted_iota(jnp.int32, (rows, total), 1)
    hit = (target == column(obs_t[mine, :])).astype(F32).T.astype(BF16)
    onehot[...] = jnp.concatenate([hit, hit], axis=1)
    for step in range(STEPS):
        inc[step] = inc_ref[:, step, :]

    def repeat(a):
        return jnp.broadcast_to(a[:, None, :], (patches, loc, src)).reshape(rows, src)

    def prepare(step):
        all_of(step, hrecv, h_send_sem, h_recv_sem).wait_recv()
        acc = hsend[step, slab].astype(F32)
        for off in range(1, n_slab):
            acc = acc + hrecv[step, off].astype(F32)
        for d in range(2, step + 1):
            acc = acc + recent_w[d] * repeat(amps[step - d])
        pre[...] = acc

    for load in loads:
        load.wait()

    prepare(0)

    for step in range(STEPS):
        driven = pre[...]
        if step > 0:
            driven = driven + recent_w[1] * repeat(amps[step - 1])
        pre[...] = driven

        def couple(p, carry):
            at = pl.ds(pl.multiple_of(p * 2 * loc, 2 * loc), 2 * loc)
            coupled[at, :] = own_blocks(pre[at, :], coup[2 * p], coup[2 * p + 1])
            return carry

        lax.fori_loop(0, patches // 2, couple, 0, unroll=True)
        whole = coupled[...]
        high = whole.astype(BF16)
        low = (whole - high.astype(F32)).astype(BF16)
        both = jnp.concatenate([high, low], axis=0)
        field = jnp.dot(onehot[...], both, preferred_element_type=F32)
        fsend[step] = field.astype(BF16).reshape(n_patch, patches, src)
        for off in range(n_patch - 1, 0, -1):
            field_copy(step, off).start()
        if step == 0:
            share_of_steps(list(range(2, STEPS)))
        all_of(step, frecv, f_send_sem, f_recv_sem).wait_recv()
        share = fsend[step, me].astype(F32)
        for off in range(1, n_patch):
            share = share + frecv[step, off].astype(F32)
        zbuf[step, 0] = share.astype(BF16)
        for off in range(n_slab - 1, 0, -1):
            slab_copy(step, off).start()
        if step + 1 < STEPS:
            prepare(step + 1)
        all_of(step, zbuf, z_send_sem, z_recv_sem).wait_recv()
        if step + 2 < STEPS:
            send_hist(step + 2)
        scattered = zbuf[step, lax.rem(slab, n_slab)].astype(F32)
        for t in range(1, n_slab):
            scattered = scattered + zbuf[step, lax.rem(slab + n_slab - t, n_slab)].astype(F32)
        drive = inc[step] - scattered
        amp = own_blocks(drive, inv[0], inv[1]).astype(BF16)
        out_ref[step] = amp
        amps[step] = amp.astype(F32)

    for step in range(STEPS):
        all_of(step, hsend, h_send_sem, h_recv_sem).wait_send()
        all_of(step, fsend, f_send_sem, f_recv_sem).wait_send()
        all_of(step, zbuf, z_send_sem, z_recv_sem).wait_send()


def on_device(n_patch, n_slab, history, interp_weights, pair_table, coupling, self_inverse, incident):
    patches, slab_len, src = history.shape
    pairs = pair_table.shape[1]
    loc = coupling.shape[1]
    rows = patches * loc
    total = n_patch * patches
    group = patches // 2
    vmem = pl.BlockSpec(memory_space=pltpu.VMEM)
    hbm = pl.BlockSpec(memory_space=pltpu.HBM)
    dma = pltpu.SemaphoreType.DMA
    out = pl.pallas_call(
        functools.partial(march, n_patch, n_slab),
        out_shape=pltpu.VMEM((STEPS, patches, src), BF16),
        in_specs=[hbm] * 6,
        out_specs=vmem,
        scratch_shapes=[
            pltpu.VMEM((patches, slab_len, src), BF16),
            pltpu.VMEM((patches, WMAX, pairs), BF16),
            pltpu.VMEM((3, patches, pairs), jnp.int32),
            pltpu.VMEM((patches, STEPS, src), F32),
            pltpu.VMEM((patches, loc * src, src), BF16),
            pltpu.VMEM((patches // group, group * src, src), BF16),
            pltpu.VMEM((pairs, patches), jnp.int32),
            pltpu.VMEM((pairs, patches), jnp.int32),
            pltpu.VMEM((WMAX, pairs, patches), F32),
            pltpu.VMEM((STEPS, rows, src), F32),
            pltpu.VMEM((total, 2 * rows), BF16),
            pltpu.VMEM((STEPS, patches, src), F32),
            pltpu.VMEM((STEPS, patches, src), F32),
            pltpu.VMEM((rows, src), F32),
            pltpu.VMEM((rows, src), F32),
            pltpu.VMEM((STEPS, n_slab, rows, src), BF16),
            pltpu.VMEM((STEPS, n_slab, rows, src), BF16),
            pltpu.VMEM((STEPS, n_patch, patches, src), BF16),
            pltpu.VMEM((STEPS, n_patch, patches, src), BF16),
            pltpu.VMEM((STEPS, n_slab, patches, src), BF16),
            dma((9,)),
            dma((STEPS,)),
            dma((STEPS,)),
            dma((STEPS,)),
            dma((STEPS,)),
            dma((STEPS,)),
            dma((STEPS,)),
        ],
        compiler_params=pltpu.CompilerParams(
            collective_id=0, has_side_effects=True, vmem_limit_bytes=62 * 1024 * 1024
        ),
    )(
        history,
        interp_weights.transpose(0, 2, 1),
        pair_table.transpose(2, 0, 1),
        coupling.reshape(patches, loc * src, src),
        self_inverse.reshape(patches // group, group * src, src),
        incident,
    )
    return out.transpose(1, 0, 2)


def solution(mesh):
    in_specs = (
        P("patch", "slab", None),
        P("patch", None, None),
        P("patch", None, None),
        P("patch", "slab", None, None),
        P("patch", None, None),
        P("patch", None, None),
    )
    out_specs = P("patch", None, None)
    return jax.shard_map(
        functools.partial(on_device, mesh.shape["patch"], mesh.shape["slab"]),
        mesh=mesh,
        in_specs=in_specs,
        out_specs=out_specs,
        check_vma=False,
    )
```

```python
import functools

import jax
import jax.numpy as jnp
from jax import lax
from jax.experimental import pallas as pl
from jax.experimental.pallas import tpu as pltpu
from jax.sharding import PartitionSpec as P

WMAX = 4
STEPS = 4
MESH = pl.DeviceIdType.MESH
F32 = jnp.float32
BF16 = jnp.bfloat16


def own_blocks(x, m):
    rows, src = x.shape
    half = rows // 2
    wide = jnp.concatenate([x, x], axis=1)
    row = lax.broadcasted_iota(jnp.int32, wide.shape, 0)
    lane = lax.broadcasted_iota(jnp.int32, wide.shape, 1)
    wide = jnp.where((row < half) == (lane < src), wide, 0.0).astype(BF16)
    full = jnp.dot(wide, m, preferred_element_type=F32)
    row = lax.rem(lax.broadcasted_iota(jnp.int32, (rows, src), 0), half)
    out = full[:, :src]
    for r in range(1, half):
        out = jnp.where(row == r, full[:, r * src : (r + 1) * src], out)
    return out


def march(
    n_patch,
    n_slab,
    hist_hbm,
    w_hbm,
    pt_hbm,
    coup_hbm,
    inv_hbm,
    inc_hbm,
    out_ref,
    hist_ref,
    w_ref,
    pt_ref,
    inc_ref,
    coup,
    inv,
    coup_t,
    inv_t,
    first_t,
    obs_t,
    wm,
    recent_w,
    onehot,
    inc,
    amps,
    pre,
    coupled,
    hsend,
    hrecv,
    fsend,
    frecv,
    zbuf,
    local_sem,
    h_send_sem,
    h_recv_sem,
    f_send_sem,
    f_recv_sem,
    z_send_sem,
    z_recv_sem,
):
    patches, slab_len, src = hist_ref.shape
    pairs = pt_ref.shape[2]
    loc = pairs // n_slab
    rows = patches * loc
    total = n_patch * patches
    me = lax.axis_index("patch")
    slab = lax.axis_index("slab")

    def patch_peer(off):
        return lax.rem(me + off, n_patch)

    def slab_peer(off):
        return lax.rem(slab + off, n_slab)

    small = [(pt_hbm, pt_ref), (w_hbm, w_ref), (hist_hbm, hist_ref), (inc_hbm, inc_ref)]
    small = [
        pltpu.make_async_copy(src_hbm, dst, local_sem.at[c])
        for c, (src_hbm, dst) in enumerate(small)
    ]
    for load in small:
        load.start()

    barrier = pltpu.get_barrier_semaphore()
    for off in range(1, n_patch):
        pl.semaphore_signal(
            barrier, inc=1, device_id={"patch": patch_peer(off), "slab": slab}, device_id_type=MESH
        )
    for off in range(1, n_slab):
        pl.semaphore_signal(
            barrier, inc=1, device_id={"patch": me, "slab": slab_peer(off)}, device_id_type=MESH
        )

    parts = 4
    size = patches // parts
    loads = [
        pltpu.make_async_copy(
            coup_hbm.at[pl.ds(c * size, size)],
            coup.at[pl.ds(c * size, size)],
            local_sem.at[len(small) + c],
        )
        for c in range(parts)
    ]
    loads.append(pltpu.make_async_copy(inv_hbm, inv, local_sem.at[len(small) + parts]))
    for load in loads:
        load.start()

    lane = lax.broadcasted_iota(jnp.int32, (pairs, slab_len), 1) + (slab * slab_len + 1)

    def stored_share(p, steps):
        shift = lane - first_t[:, p : p + 1]
        taps = [wm[j, :, p : p + 1] for j in range(WMAX)]
        hits = []
        for step in steps:
            hit = jnp.zeros((pairs, slab_len), F32)
            for j in range(WMAX):
                hit = jnp.where(shift == j - step, taps[j], hit)
            hits.append(hit)
        hit = hits[0] if len(hits) == 1 else jnp.concatenate(hits, axis=0)
        return jnp.dot(hit.astype(BF16), hist_ref[p], preferred_element_type=F32)

    def share_of_steps(steps, first_patch=0, last_patch=patches):
        for i in range(first_patch, last_patch, 2):
            a = stored_share(i, steps)
            b = stored_share(i + 1, steps)
            for k, step in enumerate(steps):
                for d in range(n_slab):
                    r = k * pairs + d * loc
                    both = jnp.concatenate([a[r : r + loc], b[r : r + loc]], axis=0)
                    hsend[step, d, i * loc : (i + 2) * loc, :] = both.astype(BF16)

    def hist_copy(step, off, half):
        dest = slab_peer(off)
        part = pl.ds(half * (rows // 2), rows // 2)
        return pltpu.make_async_remote_copy(
            src_ref=hsend.at[step, dest, part],
            dst_ref=hrecv.at[step, off, part],
            send_sem=h_send_sem.at[step, half],
            recv_sem=h_recv_sem.at[step, half],
            device_id={"patch": me, "slab": dest},
            device_id_type=MESH,
        )

    def field_copy(step, off):
        dest = patch_peer(off)
        return pltpu.make_async_remote_copy(
            src_ref=fsend.at[step, dest],
            dst_ref=frecv.at[step, off],
            send_sem=f_send_sem.at[step],
            recv_sem=f_recv_sem.at[step],
            device_id={"patch": dest, "slab": slab},
            device_id_type=MESH,
        )

    def slab_copy(step, off):
        return pltpu.make_async_remote_copy(
            src_ref=zbuf.at[step, 0],
            dst_ref=zbuf.at[step, off],
            send_sem=z_send_sem.at[step],
            recv_sem=z_recv_sem.at[step],
            device_id={"patch": me, "slab": slab_peer(off)},
            device_id_type=MESH,
        )

    def all_of(step, ref, send_sem, recv_sem):
        slots = ref.at[step, pl.ds(1, ref.shape[1] - 1)]
        return pltpu.make_async_remote_copy(
            src_ref=slots,
            dst_ref=slots,
            send_sem=send_sem.at[step],
            recv_sem=recv_sem.at[step],
            device_id={"patch": me, "slab": slab_peer(1)},
            device_id_type=MESH,
        )

    small[0].wait()
    small[1].wait()
    obs_t[...] = pt_ref[0].T
    first_t[...] = pt_ref[1].T
    band_t = pt_ref[2].T
    weights = w_ref[...].astype(F32)
    for j in range(WMAX):
        wm[j] = jnp.where(j < band_t, weights[:, j, :].T, 0.0)
    small[2].wait()
    small[3].wait()
    share_of_steps([0], 0, patches // 2)

    pl.semaphore_wait(barrier, n_patch + n_slab - 2)

    def send_hist(step, half):
        for off in range(n_slab - 1, 0, -1):
            hist_copy(step, off, half).start()

    def hist_of(step, half):
        part = pl.ds(half * (rows // 2), rows // 2)
        slots = hrecv.at[step, pl.ds(1, n_slab - 1), part]
        return pltpu.make_async_remote_copy(
            src_ref=slots,
            dst_ref=slots,
            send_sem=h_send_sem.at[step, half],
            recv_sem=h_recv_sem.at[step, half],
            device_id={"patch": me, "slab": slab_peer(1)},
            device_id_type=MESH,
        )

    send_hist(0, 0)
    share_of_steps([0], patches // 2)
    send_hist(0, 1)
    share_of_steps([1])
    for half in range(2):
        send_hist(1, half)

    mine = pl.ds(pl.multiple_of(slab * loc, loc), loc)

    def column(x):
        return jnp.concatenate([x[:, p : p + 1] for p in range(patches)], axis=0)

    first = column(first_t[mine, :])
    taps = [column(wm[j, mine, :]) for j in range(min(WMAX, STEPS - 1))]
    for d in range(1, STEPS):
        acc = jnp.zeros((rows, 1), F32)
        for j in range(min(WMAX, d)):
            acc = jnp.where(first == d - j, taps[j], acc)
        recent_w[d] = jnp.broadcast_to(acc, (rows, src))
    target = lax.broadcasted_iota(jnp.int32, (rows, total), 1)
    hit = (target == column(obs_t[mine, :])).astype(F32).T.astype(BF16)
    onehot[...] = jnp.concatenate([hit, hit], axis=1)
    for step in range(STEPS):
        inc[step] = inc_ref[:, step, :]

    def repeat(a):
        return jnp.broadcast_to(a[:, None, :], (patches, loc, src)).reshape(rows, src)

    def prepare(step, half):
        hist_of(step, half).wait_recv()
        part = pl.ds(half * (rows // 2), rows // 2)
        acc = hsend[step, slab, part, :].astype(F32)
        for off in range(1, n_slab):
            acc = acc + hrecv[step, off, part, :].astype(F32)
        for d in range(2, step + 1):
            acc = acc + recent_w[d, part, :] * repeat(amps[step - d])[part.start : part.start + part.size]
        pre[part, :] = acc

    for load in loads:
        load.wait()

    def turn(stored, turned):
        pairs_of, _, width = turned.shape
        for g in range(pairs_of):
            for h in range(2):
                for r in range(width // src):
                    block = stored[2 * g + h, r * src : (r + 1) * src, :]
                    turned[g, h * src : (h + 1) * src, r * src : (r + 1) * src] = block.T

    turn(coup, coup_t)
    turn(inv, inv_t)

    for step in range(STEPS):
        if step > 0:
            pre[...] = pre[...] + recent_w[1] * repeat(amps[step - 1])

        def couple(p, carry):
            at = pl.ds(pl.multiple_of(p * 2 * loc, 2 * loc), 2 * loc)
            coupled[at, :] = own_blocks(pre[at, :], coup_t[p])
            return carry

        for half in range(2):
            if step == 0:
                prepare(0, half)
            lax.fori_loop(half * patches // 4, (half + 1) * patches // 4, couple, 0, unroll=True)
        whole = coupled[...]
        high = whole.astype(BF16)
        low = (whole - high.astype(F32)).astype(BF16)
        both = jnp.concatenate([high, low], axis=0)
        field = jnp.dot(onehot[...], both, preferred_element_type=F32)
        fsend[step] = field.astype(BF16).reshape(n_patch, patches, src)
        for off in range(n_patch - 1, 0, -1):
            field_copy(step, off).start()
        if step == 0:
            share_of_steps(list(range(2, STEPS)))
        all_of(step, frecv, f_send_sem, f_recv_sem).wait_recv()
        share = fsend[step, me].astype(F32)
        for off in range(1, n_patch):
            share = share + frecv[step, off].astype(F32)
        zbuf[step, 0] = share.astype(BF16)
        for off in range(n_slab - 1, 0, -1):
            slab_copy(step, off).start()
        if step + 1 < STEPS:
            for half in range(2):
                prepare(step + 1, half)
        all_of(step, zbuf, z_send_sem, z_recv_sem).wait_recv()
        if step + 2 < STEPS:
            for half in range(2):
                send_hist(step + 2, half)
        scattered = zbuf[step, lax.rem(slab, n_slab)].astype(F32)
        for t in range(1, n_slab):
            scattered = scattered + zbuf[step, lax.rem(slab + n_slab - t, n_slab)].astype(F32)
        drive = inc[step] - scattered
        amp = own_blocks(drive, inv_t[0]).astype(BF16)
        out_ref[step] = amp
        amps[step] = amp.astype(F32)

    for step in range(STEPS):
        for half in range(2):
            hist_of(step, half).wait_send()
        all_of(step, fsend, f_send_sem, f_recv_sem).wait_send()
        all_of(step, zbuf, z_send_sem, z_recv_sem).wait_send()


def on_device(n_patch, n_slab, history, interp_weights, pair_table, coupling, self_inverse, incident):
    patches, slab_len, src = history.shape
    pairs = pair_table.shape[1]
    loc = coupling.shape[1]
    rows = patches * loc
    total = n_patch * patches
    group = patches // 2
    vmem = pl.BlockSpec(memory_space=pltpu.VMEM)
    hbm = pl.BlockSpec(memory_space=pltpu.HBM)
    dma = pltpu.SemaphoreType.DMA
    out = pl.pallas_call(
        functools.partial(march, n_patch, n_slab),
        out_shape=pltpu.VMEM((STEPS, patches, src), BF16),
        in_specs=[hbm] * 6,
        out_specs=vmem,
        scratch_shapes=[
            pltpu.VMEM((patches, slab_len, src), BF16),
            pltpu.VMEM((patches, WMAX, pairs), BF16),
            pltpu.VMEM((3, patches, pairs), jnp.int32),
            pltpu.VMEM((patches, STEPS, src), F32),
            pltpu.VMEM((patches, loc * src, src), BF16),
            pltpu.VMEM((patches // group, group * src, src), BF16),
            pltpu.VMEM((patches // 2, 2 * src, loc * src), BF16),
            pltpu.VMEM((1, 2 * src, group * src), BF16),
            pltpu.VMEM((pairs, patches), jnp.int32),
            pltpu.VMEM((pairs, patches), jnp.int32),
            pltpu.VMEM((WMAX, pairs, patches), F32),
            pltpu.VMEM((STEPS, rows, src), F32),
            pltpu.VMEM((total, 2 * rows), BF16),
            pltpu.VMEM((STEPS, patches, src), F32),
            pltpu.VMEM((STEPS, patches, src), F32),
            pltpu.VMEM((rows, src), F32),
            pltpu.VMEM((rows, src), F32),
            pltpu.VMEM((STEPS, n_slab, rows, src), BF16),
            pltpu.VMEM((STEPS, n_slab, rows, src), BF16),
            pltpu.VMEM((STEPS, n_patch, patches, src), BF16),
            pltpu.VMEM((STEPS, n_patch, patches, src), BF16),
            pltpu.VMEM((STEPS, n_slab, patches, src), BF16),
            dma((9,)),
            dma((STEPS, 2)),
            dma((STEPS, 2)),
            dma((STEPS,)),
            dma((STEPS,)),
            dma((STEPS,)),
            dma((STEPS,)),
        ],
        compiler_params=pltpu.CompilerParams(
            collective_id=0, has_side_effects=True, vmem_limit_bytes=62 * 1024 * 1024
        ),
    )(
        history,
        interp_weights.transpose(0, 2, 1),
        pair_table.transpose(2, 0, 1),
        coupling.reshape(patches, loc * src, src),
        self_inverse.reshape(patches // group, group * src, src),
        incident,
    )
    return out.transpose(1, 0, 2)


def solution(mesh):
    in_specs = (
        P("patch", "slab", None),
        P("patch", None, None),
        P("patch", None, None),
        P("patch", "slab", None, None),
        P("patch", None, None),
        P("patch", None, None),
    )
    out_specs = P("patch", None, None)
    return jax.shard_map(
        functools.partial(on_device, mesh.shape["patch"], mesh.shape["slab"]),
        mesh=mesh,
        in_specs=in_specs,
        out_specs=out_specs,
        check_vma=False,
    )
```

```python
import functools

import jax
import jax.numpy as jnp
from jax import lax
from jax.experimental import pallas as pl
from jax.experimental.pallas import tpu as pltpu
from jax.sharding import PartitionSpec as P

WMAX = 4
STEPS = 4
MESH = pl.DeviceIdType.MESH
F32 = jnp.float32
BF16 = jnp.bfloat16


def own_blocks(x, m):
    rows, src = x.shape
    half = rows // 2
    wide = jnp.concatenate([x, x], axis=1)
    row = lax.broadcasted_iota(jnp.int32, wide.shape, 0)
    lane = lax.broadcasted_iota(jnp.int32, wide.shape, 1)
    wide = jnp.where((row < half) == (lane < src), wide, 0.0).astype(BF16)
    full = jnp.dot(wide, m, preferred_element_type=F32)
    row = lax.rem(lax.broadcasted_iota(jnp.int32, (rows, src), 0), half)
    out = full[:, :src]
    for r in range(1, half):
        out = jnp.where(row == r, full[:, r * src : (r + 1) * src], out)
    return out


def march(
    n_patch,
    n_slab,
    hist_hbm,
    w_hbm,
    pt_hbm,
    coup_hbm,
    inv_hbm,
    inc_hbm,
    out_ref,
    hist_ref,
    w_ref,
    pt_ref,
    inc_ref,
    coup,
    inv,
    coup_t,
    inv_t,
    first_t,
    obs_t,
    wm,
    recent_w,
    onehot,
    inc,
    amps,
    pre,
    coupled,
    folded,
    ready,
    hsend,
    hrecv,
    fsend,
    frecv,
    zbuf,
    local_sem,
    h_send_sem,
    h_recv_sem,
    f_send_sem,
    f_recv_sem,
    z_send_sem,
    z_recv_sem,
):
    patches, slab_len, src = hist_ref.shape
    pairs = pt_ref.shape[2]
    loc = pairs // n_slab
    rows = patches * loc
    total = n_patch * patches
    me = lax.axis_index("patch")
    slab = lax.axis_index("slab")

    def patch_peer(off):
        return lax.rem(me + off, n_patch)

    def slab_peer(off):
        return lax.rem(slab + off, n_slab)

    small = [(pt_hbm, pt_ref), (w_hbm, w_ref), (hist_hbm, hist_ref), (inc_hbm, inc_ref)]
    small = [
        pltpu.make_async_copy(src_hbm, dst, local_sem.at[c])
        for c, (src_hbm, dst) in enumerate(small)
    ]
    for load in small:
        load.start()

    barrier = pltpu.get_barrier_semaphore()
    for off in range(1, n_patch):
        pl.semaphore_signal(
            barrier, inc=1, device_id={"patch": patch_peer(off), "slab": slab}, device_id_type=MESH
        )
    for off in range(1, n_slab):
        pl.semaphore_signal(
            barrier, inc=1, device_id={"patch": me, "slab": slab_peer(off)}, device_id_type=MESH
        )

    parts = 4
    size = patches // parts
    loads = [
        pltpu.make_async_copy(
            coup_hbm.at[pl.ds(c * size, size)],
            coup.at[pl.ds(c * size, size)],
            local_sem.at[len(small) + c],
        )
        for c in range(parts)
    ]
    loads.append(pltpu.make_async_copy(inv_hbm, inv, local_sem.at[len(small) + parts]))
    for load in loads:
        load.start()

    lane = lax.broadcasted_iota(jnp.int32, (pairs, slab_len), 1) + (slab * slab_len + 1)

    def stored_share(p, steps):
        shift = lane - first_t[:, p : p + 1]
        taps = [wm[j, :, p : p + 1] for j in range(WMAX)]
        hits = []
        for step in steps:
            hit = jnp.zeros((pairs, slab_len), F32)
            for j in range(WMAX):
                hit = jnp.where(shift == j - step, taps[j], hit)
            hits.append(hit)
        hit = hits[0] if len(hits) == 1 else jnp.concatenate(hits, axis=0)
        return jnp.dot(hit.astype(BF16), hist_ref[p], preferred_element_type=F32)

    def share_of_steps(steps, first_patch=0, last_patch=patches):
        for i in range(first_patch, last_patch, 2):
            a = stored_share(i, steps)
            b = stored_share(i + 1, steps)
            for k, step in enumerate(steps):
                for d in range(n_slab):
                    r = k * pairs + d * loc
                    both = jnp.concatenate([a[r : r + loc], b[r : r + loc]], axis=0)
                    hsend[step, d, i * loc : (i + 2) * loc, :] = both.astype(BF16)

    def hist_copy(step, off, half):
        dest = slab_peer(off)
        part = pl.ds(half * (rows // 2), rows // 2)
        return pltpu.make_async_remote_copy(
            src_ref=hsend.at[step, dest, part],
            dst_ref=hrecv.at[step, off, part],
            send_sem=h_send_sem.at[step, half],
            recv_sem=h_recv_sem.at[step, half],
            device_id={"patch": me, "slab": dest},
            device_id_type=MESH,
        )

    def field_copy(step, off):
        dest = patch_peer(off)
        return pltpu.make_async_remote_copy(
            src_ref=fsend.at[step, dest],
            dst_ref=frecv.at[step, off],
            send_sem=f_send_sem.at[step],
            recv_sem=f_recv_sem.at[step],
            device_id={"patch": dest, "slab": slab},
            device_id_type=MESH,
        )

    def slab_copy(step, off):
        return pltpu.make_async_remote_copy(
            src_ref=zbuf.at[step, 0],
            dst_ref=zbuf.at[step, off],
            send_sem=z_send_sem.at[step],
            recv_sem=z_recv_sem.at[step],
            device_id={"patch": me, "slab": slab_peer(off)},
            device_id_type=MESH,
        )

    def all_of(step, ref, send_sem, recv_sem):
        slots = ref.at[step, pl.ds(1, ref.shape[1] - 1)]
        return pltpu.make_async_remote_copy(
            src_ref=slots,
            dst_ref=slots,
            send_sem=send_sem.at[step],
            recv_sem=recv_sem.at[step],
            device_id={"patch": me, "slab": slab_peer(1)},
            device_id_type=MESH,
        )

    small[0].wait()
    small[1].wait()
    obs_t[...] = pt_ref[0].T
    first_t[...] = pt_ref[1].T
    band_t = pt_ref[2].T
    weights = w_ref[...].astype(F32)
    for j in range(WMAX):
        wm[j] = jnp.where(j < band_t, weights[:, j, :].T, 0.0)
    small[2].wait()
    small[3].wait()
    share_of_steps([0], 0, patches // 2)

    pl.semaphore_wait(barrier, n_patch + n_slab - 2)

    def send_hist(step, half):
        for off in range(n_slab - 1, 0, -1):
            hist_copy(step, off, half).start()

    def hist_of(step, half):
        part = pl.ds(half * (rows // 2), rows // 2)
        slots = hrecv.at[step, pl.ds(1, n_slab - 1), part]
        return pltpu.make_async_remote_copy(
            src_ref=slots,
            dst_ref=slots,
            send_sem=h_send_sem.at[step, half],
            recv_sem=h_recv_sem.at[step, half],
            device_id={"patch": me, "slab": slab_peer(1)},
            device_id_type=MESH,
        )

    send_hist(0, 0)
    share_of_steps([0], patches // 2)
    send_hist(0, 1)
    share_of_steps([1])
    for half in range(2):
        send_hist(1, half)

    mine = pl.ds(pl.multiple_of(slab * loc, loc), loc)

    def column(x):
        return jnp.concatenate([x[:, p : p + 1] for p in range(patches)], axis=0)

    first = column(first_t[mine, :])
    taps = [column(wm[j, mine, :]) for j in range(min(WMAX, STEPS - 1))]
    for d in range(1, STEPS):
        acc = jnp.zeros((rows, 1), F32)
        for j in range(min(WMAX, d)):
            acc = jnp.where(first == d - j, taps[j], acc)
        recent_w[d] = jnp.broadcast_to(acc, (rows, src))
    target = lax.broadcasted_iota(jnp.int32, (rows, total), 1)
    hit = (target == column(obs_t[mine, :])).astype(F32).T.astype(BF16)
    onehot[...] = jnp.concatenate([hit, hit], axis=1)
    for step in range(STEPS):
        inc[step] = inc_ref[:, step, :]

    def repeat(a):
        return jnp.broadcast_to(a[:, None, :], (patches, loc, src)).reshape(rows, src)

    def prepare(step, half):
        hist_of(step, half).wait_recv()
        part = pl.ds(half * (rows // 2), rows // 2)
        acc = hsend[step, slab, part, :].astype(F32)
        for off in range(1, n_slab):
            acc = acc + hrecv[step, off, part, :].astype(F32)
        for d in range(2, step + 1):
            acc = acc + recent_w[d, part, :] * repeat(amps[step - d])[part.start : part.start + part.size]
        pre[part, :] = acc

    for load in loads:
        load.wait()

    def turn(stored, turned):
        pairs_of, _, width = turned.shape
        for g in range(pairs_of):
            for h in range(2):
                for r in range(width // src):
                    block = stored[2 * g + h, r * src : (r + 1) * src, :]
                    turned[g, h * src : (h + 1) * src, r * src : (r + 1) * src] = block.T

    turn(coup, coup_t)
    turn(inv, inv_t)

    def couple(matrices, into, begin, end):
        def one(g, carry):
            at = pl.ds(pl.multiple_of(g * 2 * loc, 2 * loc), 2 * loc)
            into[at, :] = own_blocks(pre[at, :], matrices[g])
            return carry

        lax.fori_loop(begin, end, one, 0, unroll=True)

    def fold():
        count = patches // 2
        for p in range(patches):
            h, r = p // count, p % count
            left = inv_t[0, h * src : (h + 1) * src, r * src : (r + 1) * src]
            at = pl.ds((p % 2) * src, src)
            product = jnp.dot(left, coup_t[p // 2, at, :], preferred_element_type=F32)
            folded[p // 2, at, :] = product.astype(BF16)

    def finish(step, drive):
        amp = own_blocks(drive, inv_t[0]).astype(BF16)
        out_ref[step] = amp
        amps[step] = amp.astype(F32)

    drive = None
    for step in range(STEPS):
        if step > 0:
            pre[...] = repeat(drive)
            couple(folded, coupled, 0, patches // 2)
            whole = ready[...] + recent_w[1] * coupled[...]
        else:
            for half in range(2):
                prepare(0, half)
                couple(coup_t, coupled, half * patches // 4, (half + 1) * patches // 4)
            whole = coupled[...]
        high = whole.astype(BF16)
        low = (whole - high.astype(F32)).astype(BF16)
        both = jnp.concatenate([high, low], axis=0)
        field = jnp.dot(onehot[...], both, preferred_element_type=F32)
        fsend[step] = field.astype(BF16).reshape(n_patch, patches, src)
        for off in range(n_patch - 1, 0, -1):
            field_copy(step, off).start()
        if step == 0:
            fold()
        else:
            finish(step - 1, drive)
        all_of(step, frecv, f_send_sem, f_recv_sem).wait_recv()
        share = fsend[step, me].astype(F32)
        for off in range(1, n_patch):
            share = share + frecv[step, off].astype(F32)
        zbuf[step, 0] = share.astype(BF16)
        for off in range(n_slab - 1, 0, -1):
            slab_copy(step, off).start()
        if step == 0:
            share_of_steps(list(range(2, STEPS)))
        if step + 1 < STEPS:
            for half in range(2):
                prepare(step + 1, half)
            couple(coup_t, ready, 0, patches // 2)
        all_of(step, zbuf, z_send_sem, z_recv_sem).wait_recv()
        if step + 2 < STEPS:
            for half in range(2):
                send_hist(step + 2, half)
        scattered = zbuf[step, lax.rem(slab, n_slab)].astype(F32)
        for t in range(1, n_slab):
            scattered = scattered + zbuf[step, lax.rem(slab + n_slab - t, n_slab)].astype(F32)
        drive = (inc[step] - scattered).astype(BF16).astype(F32)
    finish(STEPS - 1, drive)

    for step in range(STEPS):
        for half in range(2):
            hist_of(step, half).wait_send()
        all_of(step, fsend, f_send_sem, f_recv_sem).wait_send()
        all_of(step, zbuf, z_send_sem, z_recv_sem).wait_send()


def on_device(n_patch, n_slab, history, interp_weights, pair_table, coupling, self_inverse, incident):
    patches, slab_len, src = history.shape
    pairs = pair_table.shape[1]
    loc = coupling.shape[1]
    rows = patches * loc
    total = n_patch * patches
    group = patches // 2
    vmem = pl.BlockSpec(memory_space=pltpu.VMEM)
    hbm = pl.BlockSpec(memory_space=pltpu.HBM)
    dma = pltpu.SemaphoreType.DMA
    out = pl.pallas_call(
        functools.partial(march, n_patch, n_slab),
        out_shape=pltpu.VMEM((STEPS, patches, src), BF16),
        in_specs=[hbm] * 6,
        out_specs=vmem,
        scratch_shapes=[
            pltpu.VMEM((patches, slab_len, src), BF16),
            pltpu.VMEM((patches, WMAX, pairs), BF16),
            pltpu.VMEM((3, patches, pairs), jnp.int32),
            pltpu.VMEM((patches, STEPS, src), F32),
            pltpu.VMEM((patches, loc * src, src), BF16),
            pltpu.VMEM((patches // group, group * src, src), BF16),
            pltpu.VMEM((patches // 2, 2 * src, loc * src), BF16),
            pltpu.VMEM((1, 2 * src, group * src), BF16),
            pltpu.VMEM((pairs, patches), jnp.int32),
            pltpu.VMEM((pairs, patches), jnp.int32),
            pltpu.VMEM((WMAX, pairs, patches), F32),
            pltpu.VMEM((STEPS, rows, src), F32),
            pltpu.VMEM((total, 2 * rows), BF16),
            pltpu.VMEM((STEPS, patches, src), F32),
            pltpu.VMEM((STEPS, patches, src), F32),
            pltpu.VMEM((rows, src), F32),
            pltpu.VMEM((rows, src), F32),
            pltpu.VMEM((patches // 2, 2 * src, loc * src), BF16),
            pltpu.VMEM((rows, src), F32),
            pltpu.VMEM((STEPS, n_slab, rows, src), BF16),
            pltpu.VMEM((STEPS, n_slab, rows, src), BF16),
            pltpu.VMEM((STEPS, n_patch, patches, src), BF16),
            pltpu.VMEM((STEPS, n_patch, patches, src), BF16),
            pltpu.VMEM((STEPS, n_slab, patches, src), BF16),
            dma((9,)),
            dma((STEPS, 2)),
            dma((STEPS, 2)),
            dma((STEPS,)),
            dma((STEPS,)),
            dma((STEPS,)),
            dma((STEPS,)),
        ],
        compiler_params=pltpu.CompilerParams(
            collective_id=0, has_side_effects=True, vmem_limit_bytes=62 * 1024 * 1024
        ),
    )(
        history,
        interp_weights.transpose(0, 2, 1),
        pair_table.transpose(2, 0, 1),
        coupling.reshape(patches, loc * src, src),
        self_inverse.reshape(patches // group, group * src, src),
        incident,
    )
    return out.transpose(1, 0, 2)


def solution(mesh):
    in_specs = (
        P("patch", "slab", None),
        P("patch", None, None),
        P("patch", None, None),
        P("patch", "slab", None, None),
        P("patch", None, None),
        P("patch", None, None),
    )
    out_specs = P("patch", None, None)
    return jax.shard_map(
        functools.partial(on_device, mesh.shape["patch"], mesh.shape["slab"]),
        mesh=mesh,
        in_specs=in_specs,
        out_specs=out_specs,
        check_vma=False,
    )
```

```python
import functools

import jax
import jax.numpy as jnp
from jax import lax
from jax.experimental import pallas as pl
from jax.experimental.pallas import tpu as pltpu
from jax.sharding import PartitionSpec as P

WMAX = 4
STEPS = 4
MESH = pl.DeviceIdType.MESH
F32 = jnp.float32
BF16 = jnp.bfloat16


def own_blocks(x, m):
    rows, src = x.shape
    half = rows // 2
    wide = jnp.concatenate([x, x], axis=1)
    row = lax.broadcasted_iota(jnp.int32, wide.shape, 0)
    lane = lax.broadcasted_iota(jnp.int32, wide.shape, 1)
    wide = jnp.where((row < half) == (lane < src), wide, 0.0).astype(BF16)
    full = jnp.dot(wide, m, preferred_element_type=F32)
    row = lax.rem(lax.broadcasted_iota(jnp.int32, (rows, src), 0), half)
    out = full[:, :src]
    for r in range(1, half):
        out = jnp.where(row == r, full[:, r * src : (r + 1) * src], out)
    return out


def march(
    n_patch,
    n_slab,
    hist_hbm,
    w_hbm,
    pt_hbm,
    coup_hbm,
    inv_hbm,
    inc_hbm,
    out_ref,
    hist_ref,
    w_ref,
    pt_ref,
    inc_ref,
    coup,
    inv,
    coup_t,
    inv_t,
    first_t,
    obs_t,
    wm,
    recent_w,
    onehot,
    inc,
    amps,
    pre,
    coupled,
    folded,
    ready,
    hsend,
    hrecv,
    fsend,
    frecv,
    zbuf,
    local_sem,
    h_send_sem,
    h_recv_sem,
    f_send_sem,
    f_recv_sem,
    z_send_sem,
    z_recv_sem,
):
    patches, slab_len, src = hist_ref.shape
    pairs = pt_ref.shape[2]
    loc = pairs // n_slab
    rows = patches * loc
    total = n_patch * patches
    me = lax.axis_index("patch")
    slab = lax.axis_index("slab")

    def patch_peer(off):
        return lax.rem(me + off, n_patch)

    def slab_peer(off):
        return lax.rem(slab + off, n_slab)

    small = [(pt_hbm, pt_ref), (w_hbm, w_ref), (hist_hbm, hist_ref), (inc_hbm, inc_ref)]
    small = [
        pltpu.make_async_copy(src_hbm, dst, local_sem.at[c])
        for c, (src_hbm, dst) in enumerate(small)
    ]
    for load in small:
        load.start()

    barrier = pltpu.get_barrier_semaphore()
    for off in range(1, n_patch):
        pl.semaphore_signal(
            barrier, inc=1, device_id={"patch": patch_peer(off), "slab": slab}, device_id_type=MESH
        )
    for off in range(1, n_slab):
        pl.semaphore_signal(
            barrier, inc=1, device_id={"patch": me, "slab": slab_peer(off)}, device_id_type=MESH
        )

    parts = 4
    size = patches // parts
    loads = [
        pltpu.make_async_copy(
            coup_hbm.at[pl.ds(c * size, size)],
            coup.at[pl.ds(c * size, size)],
            local_sem.at[len(small) + c],
        )
        for c in range(parts)
    ]
    loads.append(pltpu.make_async_copy(inv_hbm, inv, local_sem.at[len(small) + parts]))
    for load in loads:
        load.start()

    lane = lax.broadcasted_iota(jnp.int32, (pairs, slab_len), 1) + (slab * slab_len + 1)

    def stored_share(p, steps):
        shift = lane - first_t[:, p : p + 1]
        taps = [wm[j, :, p : p + 1] for j in range(WMAX)]
        hits = []
        for step in steps:
            hit = jnp.zeros((pairs, slab_len), F32)
            for j in range(WMAX):
                hit = jnp.where(shift == j - step, taps[j], hit)
            hits.append(hit)
        hit = hits[0] if len(hits) == 1 else jnp.concatenate(hits, axis=0)
        return jnp.dot(hit.astype(BF16), hist_ref[p], preferred_element_type=F32)

    def share_of_steps(steps, first_patch=0, last_patch=patches):
        for i in range(first_patch, last_patch, 2):
            a = stored_share(i, steps)
            b = stored_share(i + 1, steps)
            for k, step in enumerate(steps):
                for d in range(n_slab):
                    r = k * pairs + d * loc
                    both = jnp.concatenate([a[r : r + loc], b[r : r + loc]], axis=0)
                    hsend[step, d, i * loc : (i + 2) * loc, :] = both.astype(BF16)

    def hist_copy(step, off, half):
        dest = slab_peer(off)
        part = pl.ds(half * (rows // 2), rows // 2)
        return pltpu.make_async_remote_copy(
            src_ref=hsend.at[step, dest, part],
            dst_ref=hrecv.at[step, off, part],
            send_sem=h_send_sem.at[step, half],
            recv_sem=h_recv_sem.at[step, half],
            device_id={"patch": me, "slab": dest},
            device_id_type=MESH,
        )

    def field_copy(step, off):
        dest = patch_peer(off)
        return pltpu.make_async_remote_copy(
            src_ref=fsend.at[step, dest],
            dst_ref=frecv.at[step, off],
            send_sem=f_send_sem.at[step],
            recv_sem=f_recv_sem.at[step],
            device_id={"patch": dest, "slab": slab},
            device_id_type=MESH,
        )

    def slab_copy(step, off):
        return pltpu.make_async_remote_copy(
            src_ref=zbuf.at[step, 0],
            dst_ref=zbuf.at[step, off],
            send_sem=z_send_sem.at[step],
            recv_sem=z_recv_sem.at[step],
            device_id={"patch": me, "slab": slab_peer(off)},
            device_id_type=MESH,
        )

    def all_of(step, ref, send_sem, recv_sem):
        slots = ref.at[step, pl.ds(1, ref.shape[1] - 1)]
        return pltpu.make_async_remote_copy(
            src_ref=slots,
            dst_ref=slots,
            send_sem=send_sem.at[step],
            recv_sem=recv_sem.at[step],
            device_id={"patch": me, "slab": slab_peer(1)},
            device_id_type=MESH,
        )

    small[0].wait()
    small[1].wait()
    obs_t[...] = pt_ref[0].T
    first_t[...] = pt_ref[1].T
    band_t = pt_ref[2].T
    weights = w_ref[...].astype(F32)
    for j in range(WMAX):
        wm[j] = jnp.where(j < band_t, weights[:, j, :].T, 0.0)
    small[2].wait()
    small[3].wait()
    share_of_steps([0], 0, patches // 2)

    pl.semaphore_wait(barrier, n_patch + n_slab - 2)

    def send_hist(step, half):
        for off in range(n_slab - 1, 0, -1):
            hist_copy(step, off, half).start()

    def hist_of(step, half):
        part = pl.ds(half * (rows // 2), rows // 2)
        slots = hrecv.at[step, pl.ds(1, n_slab - 1), part]
        return pltpu.make_async_remote_copy(
            src_ref=slots,
            dst_ref=slots,
            send_sem=h_send_sem.at[step, half],
            recv_sem=h_recv_sem.at[step, half],
            device_id={"patch": me, "slab": slab_peer(1)},
            device_id_type=MESH,
        )

    send_hist(0, 0)
    share_of_steps([0], patches // 2)
    send_hist(0, 1)
    share_of_steps([1])
    for half in range(2):
        send_hist(1, half)

    mine = pl.ds(pl.multiple_of(slab * loc, loc), loc)

    def column(x):
        return jnp.concatenate([x[:, p : p + 1] for p in range(patches)], axis=0)

    target = lax.broadcasted_iota(jnp.int32, (rows, total), 1)
    hit = (target == column(obs_t[mine, :])).astype(F32).T.astype(BF16)
    onehot[...] = jnp.concatenate([hit, hit], axis=1)

    def recent_tables():
        first = column(first_t[mine, :])
        taps = [column(wm[j, mine, :]) for j in range(min(WMAX, STEPS - 1))]
        for d in range(1, STEPS):
            acc = jnp.zeros((rows, 1), F32)
            for j in range(min(WMAX, d)):
                acc = jnp.where(first == d - j, taps[j], acc)
            recent_w[d] = jnp.broadcast_to(acc, (rows, src))
        for step in range(STEPS):
            inc[step] = inc_ref[:, step, :]

    def repeat(a):
        return jnp.broadcast_to(a[:, None, :], (patches, loc, src)).reshape(rows, src)

    def prepare(step, half):
        hist_of(step, half).wait_recv()
        part = pl.ds(half * (rows // 2), rows // 2)
        acc = hsend[step, slab, part, :].astype(F32)
        for off in range(1, n_slab):
            acc = acc + hrecv[step, off, part, :].astype(F32)
        for d in range(2, step + 1):
            acc = acc + recent_w[d, part, :] * repeat(amps[step - d])[part.start : part.start + part.size]
        pre[part, :] = acc

    for load in loads:
        load.wait()

    def turn(stored, turned):
        pairs_of, _, width = turned.shape
        for g in range(pairs_of):
            for h in range(2):
                for r in range(width // src):
                    block = stored[2 * g + h, r * src : (r + 1) * src, :]
                    turned[g, h * src : (h + 1) * src, r * src : (r + 1) * src] = block.T

    turn(coup, coup_t)

    def couple(matrices, into, begin, end):
        def one(g, carry):
            at = pl.ds(pl.multiple_of(g * 2 * loc, 2 * loc), 2 * loc)
            into[at, :] = own_blocks(pre[at, :], matrices[g])
            return carry

        lax.fori_loop(begin, end, one, 0, unroll=True)

    def fold():
        count = patches // 2
        for p in range(patches):
            h, r = p // count, p % count
            left = inv_t[0, h * src : (h + 1) * src, r * src : (r + 1) * src]
            at = pl.ds((p % 2) * src, src)
            product = jnp.dot(left, coup_t[p // 2, at, :], preferred_element_type=F32)
            folded[p // 2, at, :] = product.astype(BF16)

    def finish(step, drive):
        amp = own_blocks(drive, inv_t[0]).astype(BF16)
        out_ref[step] = amp
        amps[step] = amp.astype(F32)

    drive = None
    for step in range(STEPS):
        if step > 0:
            pre[...] = repeat(drive)
            couple(folded, coupled, 0, patches // 2)
            whole = ready[...] + recent_w[1] * coupled[...]
        else:
            for half in range(2):
                prepare(0, half)
                couple(coup_t, coupled, half * patches // 4, (half + 1) * patches // 4)
            whole = coupled[...]
        high = whole.astype(BF16)
        low = (whole - high.astype(F32)).astype(BF16)
        both = jnp.concatenate([high, low], axis=0)
        field = jnp.dot(onehot[...], both, preferred_element_type=F32)
        fsend[step] = field.astype(BF16).reshape(n_patch, patches, src)
        for off in range(n_patch - 1, 0, -1):
            field_copy(step, off).start()
        if step == 0:
            turn(inv, inv_t)
            fold()
        else:
            finish(step - 1, drive)
            if step + 2 < STEPS:
                share_of_steps([step + 2])
        all_of(step, frecv, f_send_sem, f_recv_sem).wait_recv()
        share = fsend[step, me].astype(F32)
        for off in range(1, n_patch):
            share = share + frecv[step, off].astype(F32)
        zbuf[step, 0] = share.astype(BF16)
        for off in range(n_slab - 1, 0, -1):
            slab_copy(step, off).start()
        if step == 0:
            recent_tables()
            share_of_steps([2])
        if step + 1 < STEPS:
            for half in range(2):
                prepare(step + 1, half)
            couple(coup_t, ready, 0, patches // 2)
        all_of(step, zbuf, z_send_sem, z_recv_sem).wait_recv()
        if step + 2 < STEPS:
            for half in range(2):
                send_hist(step + 2, half)
        scattered = zbuf[step, lax.rem(slab, n_slab)].astype(F32)
        for t in range(1, n_slab):
            scattered = scattered + zbuf[step, lax.rem(slab + n_slab - t, n_slab)].astype(F32)
        drive = (inc[step] - scattered).astype(BF16).astype(F32)
    finish(STEPS - 1, drive)

    for step in range(STEPS):
        for half in range(2):
            hist_of(step, half).wait_send()
        all_of(step, fsend, f_send_sem, f_recv_sem).wait_send()
        all_of(step, zbuf, z_send_sem, z_recv_sem).wait_send()


def on_device(n_patch, n_slab, history, interp_weights, pair_table, coupling, self_inverse, incident):
    patches, slab_len, src = history.shape
    pairs = pair_table.shape[1]
    loc = coupling.shape[1]
    rows = patches * loc
    total = n_patch * patches
    group = patches // 2
    vmem = pl.BlockSpec(memory_space=pltpu.VMEM)
    hbm = pl.BlockSpec(memory_space=pltpu.HBM)
    dma = pltpu.SemaphoreType.DMA
    out = pl.pallas_call(
        functools.partial(march, n_patch, n_slab),
        out_shape=pltpu.VMEM((STEPS, patches, src), BF16),
        in_specs=[hbm] * 6,
        out_specs=vmem,
        scratch_shapes=[
            pltpu.VMEM((patches, slab_len, src), BF16),
            pltpu.VMEM((patches, WMAX, pairs), BF16),
            pltpu.VMEM((3, patches, pairs), jnp.int32),
            pltpu.VMEM((patches, STEPS, src), F32),
            pltpu.VMEM((patches, loc * src, src), BF16),
            pltpu.VMEM((patches // group, group * src, src), BF16),
            pltpu.VMEM((patches // 2, 2 * src, loc * src), BF16),
            pltpu.VMEM((1, 2 * src, group * src), BF16),
            pltpu.VMEM((pairs, patches), jnp.int32),
            pltpu.VMEM((pairs, patches), jnp.int32),
            pltpu.VMEM((WMAX, pairs, patches), F32),
            pltpu.VMEM((STEPS, rows, src), F32),
            pltpu.VMEM((total, 2 * rows), BF16),
            pltpu.VMEM((STEPS, patches, src), F32),
            pltpu.VMEM((STEPS, patches, src), F32),
            pltpu.VMEM((rows, src), F32),
            pltpu.VMEM((rows, src), F32),
            pltpu.VMEM((patches // 2, 2 * src, loc * src), BF16),
            pltpu.VMEM((rows, src), F32),
            pltpu.VMEM((STEPS, n_slab, rows, src), BF16),
            pltpu.VMEM((STEPS, n_slab, rows, src), BF16),
            pltpu.VMEM((STEPS, n_patch, patches, src), BF16),
            pltpu.VMEM((STEPS, n_patch, patches, src), BF16),
            pltpu.VMEM((STEPS, n_slab, patches, src), BF16),
            dma((9,)),
            dma((STEPS, 2)),
            dma((STEPS, 2)),
            dma((STEPS,)),
            dma((STEPS,)),
            dma((STEPS,)),
            dma((STEPS,)),
        ],
        compiler_params=pltpu.CompilerParams(
            collective_id=0, has_side_effects=True, vmem_limit_bytes=62 * 1024 * 1024
        ),
    )(
        history,
        interp_weights.transpose(0, 2, 1),
        pair_table.transpose(2, 0, 1),
        coupling.reshape(patches, loc * src, src),
        self_inverse.reshape(patches // group, group * src, src),
        incident,
    )
    return out.transpose(1, 0, 2)


def solution(mesh):
    in_specs = (
        P("patch", "slab", None),
        P("patch", None, None),
        P("patch", None, None),
        P("patch", "slab", None, None),
        P("patch", None, None),
        P("patch", None, None),
    )
    out_specs = P("patch", None, None)
    return jax.shard_map(
        functools.partial(on_device, mesh.shape["patch"], mesh.shape["slab"]),
        mesh=mesh,
        in_specs=in_specs,
        out_specs=out_specs,
        check_vma=False,
    )
```
